32 devices in a mesh: gx: 16 (over z, x, core), gy: 2 (over y).
Axes of the slice: x: 2, y: 2, z: 4, core: 2. Of those that a mesh axis runs over, the one named last changes fastest.
Arguments:
- state: float32 [512, 128, 384], P('gx', 'gy'), may hold values from -3 to 3
- obs_owner: int32 [2, 4096], replicated, may hold values from 0 to 31
- obs_cell: int32 [2, 4096], replicated, may hold values from 0 to 2047
- obs_level: int32 [2, 4096], replicated, may hold values from 0 to 3
- obs_coef: float32 [2, 3, 4096], replicated, may hold values from -1 to 1
- obs_value: float32 [2, 4096], replicated, may hold values from -8 to 8
- obs_error: float32 [2, 4096], replicated, may hold values from 0.5 to 2
- pattern: int32 [16, 2, 2, 16], P('gx', 'gy'), may hold values 0 or 1
Outputs:
- analysis: float32 [512, 128, 384], P('gx', 'gy')
The draws below stay inside these ranges and needn't reach their ends.
Inputs may be any that keep to these rules, and one draw needn't show every extreme that they name: `obs_owner`: the tile numbered (its gx index) * 2 + (its gy index). `obs_cell`: cell i * 64 + j of the owner tile, i along the first dimension. `pattern`: 1 where the tile uses the block.
All inputs are finite; a program needn't handle non-finite values. Where the reference program divides by a largest or mean magnitude, that divisor is 1e-20 or more.
Results may differ from the reference program's by a relative error of at most 0.0003.
Values sent between devices are 32-bit elements; how exact they have to be, the bound alone decides.
A program may use at most 128 MiB of HBM per device.

```python
import math
import jax
import jax.numpy as jnp
import numpy as np
from jax import lax

CX = 32
CY = 64
NOBS = 4096
ENS = 32
LEV = 4
COMP = 3
NBAT = 2
OBLK = 16
NSIT = 4
TX = 16
TY = 2
TILES = 32
NX = 512
NY = 128
FEAT = 384


def touch_ends(entries, own_key, low, top_value):
    shape = entries.shape
    index_at = [jax.random.randint(jax.random.fold_in(own_key, axis), (), 0, shape[axis]) for axis in range(len(shape))]
    entries = entries.at[tuple(index_at)].set(low)
    longest = shape.index(max(shape))
    index_at[longest] = (index_at[longest] + 1) % shape[longest]
    return entries.at[tuple(index_at)].set(top_value)


def steps_of(own_key, shape, cuts, least, largest):
    loudness = 1.0
    for position, parts in cuts:
        draws = jax.random.uniform(jax.random.fold_in(jax.random.fold_in(own_key, 6), position), (parts,), jnp.float32, least / len(cuts), largest / len(cuts))
        loudness = loudness * jnp.repeat(jnp.exp(draws), shape[position] // parts).reshape((-1,) + (1,) * (len(shape) - 1 - position))
    return loudness


def cumulative_ranks(number_of, slope):
    weights = [(1 << 20) // math.isqrt(standing ** slope) + 1 for standing in range(1, number_of + 1)]
    spread = 1 + sum(weights) // (1 << 30)
    return np.cumsum(np.array([max(1, weight // spread) for weight in weights]))


def skewed_ids(own_key, extent, number_of, slope):
    grid = cumulative_ranks(number_of, slope)
    lot = jax.random.randint(jax.random.fold_in(own_key, 1), extent, 0, int(grid[number_of - 1]))
    rank = jnp.searchsorted(jnp.asarray(grid, jnp.int32), lot, side="right")
    return jax.random.permutation(jax.random.fold_in(own_key, 2), number_of)[rank].astype(jnp.int32)


def gaussian(key, dims, spread, most, cuts=(), kind=jnp.bfloat16):
    array = jax.random.normal(key, dims, jnp.float32) * spread
    if len(cuts) > 0:
        array = steps_of(key, dims, cuts, -0.22, 0.18) * array
    return jnp.clip(array, min=-most, max=most).astype(kind)


def setup_inputs(seed: int = 0) -> dict:
    arg_keys = jax.random.split(jax.random.key(seed), 9)
    return {
        "state": gaussian(arg_keys[0], (NX, NY, FEAT), 1.0, 3.0, ((0, 16), (1, 2)), jnp.float32),
        "obs_owner": touch_ends(skewed_ids(arg_keys[1], (NBAT, NOBS), TILES, 2), jax.random.fold_in(arg_keys[1], 3), 0, TILES - 1).astype(jnp.int32),
        "obs_cell": touch_ends(jax.random.randint(arg_keys[2], (NBAT, NOBS), 0, CX * CY), jax.random.fold_in(arg_keys[2], 1), 0, (CX * CY) - 1).astype(jnp.int32),
        "obs_level": touch_ends(jax.random.randint(arg_keys[3], (NBAT, NOBS), 0, LEV), jax.random.fold_in(arg_keys[3], 1), 0, LEV - 1).astype(jnp.int32),
        "obs_coef": jnp.clip(jax.random.uniform(arg_keys[4], (NBAT, COMP, NOBS), jnp.float32, -1.0, 1.0), -1.0, 1.0),
        "obs_value": gaussian(arg_keys[5], (NBAT, NOBS), 1.5, 8.0, (), jnp.float32),
        "obs_error": jnp.clip(jnp.exp(jax.random.uniform(arg_keys[6], (NBAT, NOBS), jnp.float32, math.log(0.5), math.log(2.0))), 0.5, 2.0),
        "pattern": touch_ends((jax.random.randint(arg_keys[7], (TX, TY, NBAT, OBLK), 0, 2) < 1).astype(jnp.int32), jax.random.fold_in(arg_keys[7], 1), 0, 1),
    }


courant = 0.1
diffusion = 0.08
radius_share = 0.25

def update(centre, west_cell, east_cell, south_cell, north_cell):
    speed_east = centre[:, :, 0:1]
    speed_north = centre[:, :, 1:2]
    upwind_flux = jnp.maximum(speed_east, 0.0) * (centre - west_cell) + jnp.minimum(speed_east, 0.0) * (east_cell - centre) + jnp.maximum(speed_north, 0.0) * (centre - south_cell) + jnp.minimum(speed_north, 0.0) * (north_cell - centre)
    return centre - courant * upwind_flux + diffusion * (west_cell + east_cell + (south_cell + north_cell) - 4.0 * centre)

def advance(grid_field):
    pieces = []
    for level_index in range(LEV):
        level_slab = grid_field[:, :, :, level_index * ENS:(level_index + 1) * ENS]
        pieces.append(update(level_slab, jnp.roll(level_slab, 1, axis=0), jnp.roll(level_slab, -1, axis=0), jnp.roll(level_slab, 1, axis=1), jnp.roll(level_slab, -1, axis=1)))
    return jnp.concatenate(pieces, axis=3)

def product(left, right):
    return jnp.dot(left, right, precision=lax.Precision.HIGHEST, preferred_element_type=jnp.float32)

def innovations(predicted, obs_value, obs_error):
    centre_obs = lax.optimization_barrier(jnp.mean(predicted, axis=1, keepdims=True))
    deviation = (predicted - centre_obs) / obs_error[:, None]
    innovation = (obs_value - centre_obs[:, 0]) / obs_error
    return (deviation, innovation)

def localize(owners, obs_cells, block_mask, tile_east, tile_north, span_east, span_north, tiles_north, grid_east, grid_north):
    place_east = (owners // tiles_north * span_east + obs_cells // span_north).astype(jnp.float32)
    place_north = (owners % tiles_north * span_north + obs_cells % span_north).astype(jnp.float32)
    centre_east = (tile_east * span_east).astype(jnp.float32) + (span_east - 1) / 2.0
    centre_north = (tile_north * span_north).astype(jnp.float32) + (span_north - 1) / 2.0
    gap_east = jnp.remainder(place_east - centre_east + grid_east / 2.0, grid_east) - grid_east / 2.0
    gap_north = jnp.remainder(place_north - centre_north + grid_north / 2.0, grid_north) - grid_north / 2.0
    scale_east = gap_east / (radius_share * grid_east)
    scale_north = gap_north / (radius_share * grid_north)
    weight = jnp.exp(-0.5 * (scale_east * scale_east + scale_north * scale_north))
    blocks = block_mask.shape[0]
    return (weight.reshape(blocks, -1) * block_mask.astype(jnp.float32)[:, None]).reshape(-1)

def transform(deviation, innovation, weight_obs):
    members = deviation.shape[1]
    weighted = deviation * weight_obs[:, None]
    covariance = product(weighted.T, deviation)
    projection = product(weighted.T, innovation[:, None])[:, 0]
    unit_matrix = jnp.eye(members, dtype=jnp.float32)
    system = (members - 1.0) * unit_matrix + covariance
    row_bound = jnp.max(lax.optimization_barrier(jnp.sum(jnp.abs(system), axis=1)))

    def refine(sweep_index, iterates):
        approach, inverse_root = iterates
        middle = 1.5 * unit_matrix - 0.5 * product(inverse_root, approach)
        return (product(approach, middle), product(middle, inverse_root))
    approach, inverse_root = lax.fori_loop(0, NSIT, refine, (system / row_bound, unit_matrix))
    inverse = product(inverse_root, inverse_root) / row_bound
    weights = product(inverse, projection[:, None])[:, 0]
    centring = unit_matrix - 1.0 / members
    shifts = weights[:, None] + math.sqrt(members - 1.0) * inverse_root / jnp.sqrt(row_bound)
    return 1.0 / members + product(centring, shifts)

def predict(grid_field, owners, obs_cells, levels, obs_coefs):
    place_east = owners // TY * CX + obs_cells // CY
    place_north = owners % TY * CY + obs_cells % CY
    picked = grid_field[place_east, place_north, :, levels, :]
    return obs_coefs[0][:, None] * picked[:, 0] + obs_coefs[1][:, None] * picked[:, 1] + obs_coefs[2][:, None] * picked[:, 2]

def reference(state, obs_owner, obs_cell, obs_level, obs_coef, obs_value, obs_error, pattern):
    grid_field = state.reshape(NX, NY, COMP, LEV * ENS)
    for substep in range(2):
        grid_field = advance(grid_field)
    grid_field = grid_field.reshape(NX, NY, COMP, LEV, ENS)
    for batch_index in range(NBAT):
        predicted = predict(grid_field, obs_owner[batch_index], obs_cell[batch_index], obs_level[batch_index], obs_coef[batch_index])
        deviation, innovation = innovations(predicted, obs_value[batch_index], obs_error[batch_index])

        def one_tile(tile_index):
            tile_east = tile_index // TY
            tile_north = tile_index % TY
            weight_obs = localize(obs_owner[batch_index], obs_cell[batch_index], pattern[tile_east, tile_north, batch_index], tile_east, tile_north, CX, CY, TY, NX, NY)
            return transform(deviation, innovation, weight_obs)
        all_mixes = lax.map(one_tile, jnp.arange(TILES, dtype=jnp.int32))
        tiled = grid_field.reshape(TX, CX, TY, CY, COMP * LEV, ENS)
        grid_field = jnp.einsum('aibjke,abef->aibjkf', tiled, all_mixes.reshape(TX, TY, ENS, ENS), precision=lax.Precision.HIGHEST).reshape(NX, NY, COMP, LEV, ENS)
    return grid_field.reshape(NX, NY, FEAT)
```

```python
import functools
import math

import jax
import jax.numpy as jnp
from jax import lax
from jax.experimental import pallas as pl
from jax.experimental.pallas import tpu as pltpu
from jax.sharding import PartitionSpec as P

ENS = 32
LEV = 4
COMP = 3
NSIT = 4
CHUNK = 256
LANES = 128

courant = 0.1
diffusion = 0.08
radius_share = 0.25

VMEM_LIMIT = 48 * 1024 * 1024
HIGHEST = lax.Precision.HIGHEST
F32 = jnp.float32
BF16 = jnp.bfloat16

smem = pl.BlockSpec(memory_space=pltpu.SMEM)
vmem = pl.BlockSpec(memory_space=pltpu.VMEM)


def exact_dot(left, right):
    return jnp.dot(left, right, precision=HIGHEST, preferred_element_type=F32)


def half_dot(left, right):
    return jnp.dot(left, right, preferred_element_type=F32)


def split(values):
    high = values.astype(BF16)
    low = (values - high.astype(F32)).astype(BF16)
    return high, low


def compact_kernel(nobs, tile_ref, owner_ref, order_ref, count_ref):
    me = tile_ref[0]
    step = 16
    for batch in range(2):
        base = batch * nobs

        def body(i, count):
            first = i * step
            owners = [owner_ref[base + first + k] for k in range(step)]
            for k in range(step):
                order_ref[base + count] = first + k
                count = count + jnp.where(owners[k] == me, 1, 0)
            return count

        count_ref[batch] = lax.fori_loop(0, nobs // step, body, 0)


def compact(tile, owners):
    batches, nobs = owners.shape
    return pl.pallas_call(
        functools.partial(compact_kernel, nobs),
        out_shape=(
            jax.ShapeDtypeStruct((batches * nobs,), jnp.int32),
            jax.ShapeDtypeStruct((batches,), jnp.int32),
        ),
        in_specs=[smem, smem],
        out_specs=(smem, smem),
        cost_estimate=pl.CostEstimate(flops=40_000_000, bytes_accessed=20_000_000, transcendentals=0),
    )(tile, owners.reshape(-1))


def forecast_kernel(state_ref, west_ref, east_ref, south_ref, north_ref, out_ref, wide, middle):
    nx, ny, _ = state_ref.shape
    wide[2 : nx + 2, 8 : ny + 8, :] = state_ref[...]
    wide[0:2, 8 : ny + 8, :] = west_ref[...]
    wide[nx + 2 : nx + 4, 8 : ny + 8, :] = east_ref[...]
    wide[:, 6:8, :] = south_ref[...]
    wide[:, ny + 8 : ny + 10, :] = north_ref[...]
    rows = ny + 16

    def updated(src, x, comp, up, um, vp, vm):
        lanes = slice(comp * LANES, (comp + 1) * LANES)
        centre = src[x, :, lanes]
        west = src[x - 1, :, lanes]
        east = src[x + 1, :, lanes]
        south = pltpu.roll(centre, 1, 0)
        north = pltpu.roll(centre, rows - 1, 0)
        flux = up * (centre - west) + um * (east - centre) + vp * (centre - south) + vm * (north - centre)
        return centre - courant * flux + diffusion * ((west + east) + (south + north) - 4.0 * centre)

    def speeds(src, x):
        u = src[x, :, 0:LANES]
        v = src[x, :, LANES : 2 * LANES]
        return jnp.maximum(u, 0.0), jnp.minimum(u, 0.0), jnp.maximum(v, 0.0), jnp.minimum(v, 0.0)

    def first(i, carry):
        parts = speeds(wide, i + 1)
        for comp in range(COMP):
            middle[i, :, comp * LANES : (comp + 1) * LANES] = updated(wide, i + 1, comp, *parts)
        return carry

    lax.fori_loop(0, nx + 2, first, 0)

    def second(i, carry):
        parts = speeds(middle, i + 1)
        for comp in range(COMP):
            new = updated(middle, i + 1, comp, *parts)
            out_ref[pl.ds(pl.multiple_of(i * ny, ny), ny), comp * LANES : (comp + 1) * LANES] = new[8 : ny + 8]
        return carry

    lax.fori_loop(0, nx, second, 0)


def forecast(state, west, east, south, north):
    nx, ny, feat = state.shape
    return pl.pallas_call(
        forecast_kernel,
        out_shape=jax.ShapeDtypeStruct((nx * ny, feat), F32),
        in_specs=[vmem] * 5,
        out_specs=vmem,
        scratch_shapes=[
            pltpu.VMEM((nx + 4, ny + 16, feat), F32),
            pltpu.VMEM((nx + 2, ny + 16, feat), F32),
        ],
        compiler_params=pltpu.CompilerParams(vmem_limit_bytes=VMEM_LIMIT),
    )(state, west, east, south, north)


def sums_kernel(batch, nobs, tiles, mixed, count_ref, order_ref, cell_ref, field_ref, table_ref, *rest):
    if mixed:
        mix_ref, out_ref, picked, params, total = rest
    else:
        out_ref, picked, params, total = rest
    count = count_ref[batch]
    base = batch * nobs
    total[...] = jnp.zeros_like(total)
    lane = lax.broadcasted_iota(jnp.int32, (CHUNK, LANES), 1)
    group = lane // ENS
    row = lax.broadcasted_iota(jnp.int32, (CHUNK, 1), 0)
    width = table_ref.shape[1] - LANES
    tile_of_row = lax.broadcasted_iota(jnp.int32, (width, 256), 0)
    tile_of_lane = lax.broadcasted_iota(jnp.int32, (width, 256), 1) // ENS

    def chunk(ci, carry):
        def pick(i, carry):
            for k in range(8):
                at = i * 8 + k
                place = ci * CHUNK + at
                j = jnp.where(place < count, order_ref[base + place], 0)
                picked[pl.ds(at, 1), :] = field_ref[pl.ds(cell_ref[base + j], 1), :]
                params[pl.ds(at, 1), :] = table_ref[pl.ds(j, 1), :]
            return carry

        lax.fori_loop(0, CHUNK // 8, pick, 0)
        param = params[:, 0:LANES]
        values = (
            param[:, 0:1] * picked[:, 0:LANES]
            + param[:, 1:2] * picked[:, LANES : 2 * LANES]
            + param[:, 2:3] * picked[:, 2 * LANES : 3 * LANES]
        )
        values = jnp.where(group.astype(F32) == param[:, 3:4], values, 0.0)
        values = values + pltpu.roll(values, 64, 1)
        values = values + pltpu.roll(values, 32, 1)
        if mixed:
            values = exact_dot(values, mix_ref[...])
        centre = jnp.sum(values, axis=1, keepdims=True) / float(LANES)
        inverse_error = param[:, 5:6]
        deviation = (values - centre) * inverse_error
        innovation = (param[:, 4:5] - centre) * inverse_error
        rho = jnp.where(ci * CHUNK + row < count, params[:, LANES:], 0.0)
        left = jnp.where(group == 0, deviation, jnp.where(lane == ENS, innovation, 0.0))
        high, low = split(left.T[0:48])
        both = jnp.concatenate([high, low], axis=0)
        rho_high, rho_low = split(rho)
        pair = jnp.concatenate([deviation, deviation], axis=1)
        for g in range(tiles // 8):
            spread = jnp.where(tile_of_row == tile_of_lane + g * 8, 1.0, 0.0).astype(BF16)
            weight = half_dot(rho_high, spread) + half_dot(rho_low, spread)
            right_high, right_low = split(weight * pair)
            first = half_dot(both, right_high)
            second = half_dot(high, right_low)
            total[:, g * 256 : (g + 1) * 256] += first[0:48] + first[48:96] + second
        return carry

    lax.fori_loop(0, (count + CHUNK - 1) // CHUNK, chunk, 0)
    small = lax.broadcasted_iota(jnp.int32, (8, LANES), 1) // ENS

    def pack(q, carry):
        lanes = pl.ds(pl.multiple_of(q * LANES, LANES), LANES)
        blocks = [total[8 * r : 8 * r + 8, lanes] for r in range(5)]
        for t in range(4):
            packed = jnp.zeros((8, LANES), F32)
            for r in range(4):
                moved = pltpu.roll(blocks[r], (32 * (r - t)) % LANES, 1) if r != t else blocks[r]
                packed = jnp.where(small == r, moved, packed)
            proj = pltpu.roll(blocks[4], (-32 * t) % LANES, 1) if t else blocks[4]
            out_ref[q * 4 + t, 0:8, :] = packed
            out_ref[q * 4 + t, 8:16, :] = jnp.where(small == 0, proj, 0.0)
        return carry

    lax.fori_loop(0, tiles // 4, pack, 0)


def own_sums(batch, nobs, tiles, counts, order, cells, field, table, mix=None):
    extra = [] if mix is None else [mix]
    return pl.pallas_call(
        functools.partial(sums_kernel, batch, nobs, tiles, mix is not None),
        out_shape=jax.ShapeDtypeStruct((tiles, 16, LANES), F32),
        in_specs=[smem] * 3 + [vmem] * (2 + len(extra)),
        out_specs=vmem,
        scratch_shapes=[
            pltpu.VMEM((CHUNK, COMP * LANES), F32),
            pltpu.VMEM((CHUNK, table.shape[1]), F32),
            pltpu.VMEM((48, tiles * ENS), F32),
        ],
        compiler_params=pltpu.CompilerParams(vmem_limit_bytes=VMEM_LIMIT),
    )(counts, order, cells, field, table, *extra)


def mix_kernel(tiles_east, tiles_north, x_ref, out_ref, held, send_sem, recv_sem):
    tiles = tiles_east * tiles_north
    me = lax.axis_index("gx") * tiles_north + lax.axis_index("gy")

    def device(t):
        return (t // tiles_north, lax.rem(t, tiles_north))

    barrier = pltpu.get_barrier_semaphore()

    def greet(d, carry):
        pl.semaphore_signal(
            barrier, inc=1, device_id=device(lax.rem(me + d, tiles)), device_id_type=pl.DeviceIdType.MESH
        )
        return carry

    lax.fori_loop(1, tiles, greet, 0)
    pl.semaphore_wait(barrier, tiles - 1)

    def send(d, carry):
        target = lax.rem(me + d, tiles)
        pltpu.make_async_remote_copy(
            src_ref=x_ref.at[target],
            dst_ref=held.at[d - 1],
            send_sem=send_sem,
            recv_sem=recv_sem,
            device_id=device(target),
            device_id_type=pl.DeviceIdType.MESH,
        ).start()
        return carry

    lax.fori_loop(1, tiles, send, 0)
    pltpu.make_async_copy(held, held, recv_sem).wait()
    pltpu.make_async_copy(held, held, send_sem).wait()

    total = lax.fori_loop(0, tiles - 1, lambda d, acc: acc + held[d], x_ref[me])
    top = total[0:8]
    cov = jnp.concatenate([top] + [pltpu.roll(top, LANES - 32 * r, 1) for r in range(1, 4)], axis=0)[:, 0:ENS]
    proj = total[8:9, 0:ENS]
    ri = lax.broadcasted_iota(jnp.int32, (ENS, ENS), 0)
    ci = lax.broadcasted_iota(jnp.int32, (ENS, ENS), 1)
    unit = jnp.where(ri == ci, 1.0, 0.0)
    system = (ENS - 1.0) * unit + cov
    bound = jnp.max(jnp.sum(jnp.abs(system), axis=1, keepdims=True), axis=0, keepdims=True)
    approach, root = system / bound, unit
    for sweep in range(NSIT):
        middle = 1.5 * unit - 0.5 * exact_dot(root, approach)
        approach, root = exact_dot(approach, middle), exact_dot(middle, root)
    inverse = exact_dot(root, root) / bound
    weights = jnp.sum(inverse * proj, axis=1, keepdims=True)
    shifts = weights + math.sqrt(ENS - 1.0) * root / jnp.sqrt(bound)
    mix = 1.0 / ENS + (shifts - jnp.mean(shifts, axis=0, keepdims=True))
    er = lax.broadcasted_iota(jnp.int32, (ENS, LANES), 0)
    ec = lax.broadcasted_iota(jnp.int32, (ENS, LANES), 1)
    repeated = exact_dot(mix, jnp.where(lax.rem(ec, ENS) == er, 1.0, 0.0))
    full = jnp.concatenate([repeated] * 4, axis=0)
    br = lax.broadcasted_iota(jnp.int32, (LANES, LANES), 0) // ENS
    bc = lax.broadcasted_iota(jnp.int32, (LANES, LANES), 1) // ENS
    out_ref[...] = jnp.where(br == bc, full, 0.0)


def tile_mix(tiles_east, tiles_north, sums):
    tiles = tiles_east * tiles_north
    return pl.pallas_call(
        functools.partial(mix_kernel, tiles_east, tiles_north),
        out_shape=jax.ShapeDtypeStruct((LANES, LANES), F32),
        in_specs=[vmem],
        out_specs=vmem,
        scratch_shapes=[
            pltpu.VMEM((tiles - 1, 16, LANES), F32),
            pltpu.SemaphoreType.DMA,
            pltpu.SemaphoreType.DMA,
        ],
        compiler_params=pltpu.CompilerParams(
            collective_id=0, has_side_effects=True, vmem_limit_bytes=VMEM_LIMIT
        ),
    )(sums)


def apply_kernel(field_ref, one_ref, two_ref, out_ref):
    high, low = split(exact_dot(one_ref[...], two_ref[...]))
    for comp in range(COMP):
        lanes = slice(comp * LANES, (comp + 1) * LANES)
        value_high, value_low = split(field_ref[:, lanes])
        out_ref[:, lanes] = half_dot(value_high, high) + half_dot(value_low, high) + half_dot(value_high, low)


def apply_mix(field, one, two):
    rows, feat = field.shape
    block = 512
    return pl.pallas_call(
        apply_kernel,
        out_shape=jax.ShapeDtypeStruct((rows, feat), F32),
        grid=(rows // block,),
        in_specs=[
            pl.BlockSpec((block, feat), lambda i: (i, 0)),
            pl.BlockSpec((LANES, LANES), lambda i: (0, 0)),
            pl.BlockSpec((LANES, LANES), lambda i: (0, 0)),
        ],
        out_specs=pl.BlockSpec((block, feat), lambda i: (i, 0)),
        compiler_params=pltpu.CompilerParams(vmem_limit_bytes=VMEM_LIMIT),
    )(field, one, two)


def neighbours(axis, last, initial):
    size = lax.axis_size(axis)
    up = [(i, (i + 1) % size) for i in range(size)]
    down = [(j, i) for i, j in up]
    return lax.ppermute(last, axis, up), lax.ppermute(initial, axis, down)


def distance_weights(owners, cells, span_east, span_north, tiles_east, tiles_north):
    grid_east, grid_north = span_east * tiles_east, span_north * tiles_north
    place_east = (owners // tiles_north * span_east + cells // span_north).astype(F32)[:, None]
    place_north = (owners % tiles_north * span_north + cells % span_north).astype(F32)[:, None]
    tile = jnp.arange(tiles_east * tiles_north, dtype=jnp.int32)[None, :]
    centre_east = (tile // tiles_north * span_east).astype(F32) + (span_east - 1) / 2.0
    centre_north = (tile % tiles_north * span_north).astype(F32) + (span_north - 1) / 2.0
    gap_east = place_east - centre_east
    gap_east = jnp.where(gap_east >= grid_east / 2.0, gap_east - grid_east, gap_east)
    gap_east = jnp.where(gap_east < -grid_east / 2.0, gap_east + grid_east, gap_east)
    gap_north = place_north - centre_north
    gap_north = jnp.where(gap_north >= grid_north / 2.0, gap_north - grid_north, gap_north)
    gap_north = jnp.where(gap_north < -grid_north / 2.0, gap_north + grid_north, gap_north)
    scale_east = gap_east / (radius_share * grid_east)
    scale_north = gap_north / (radius_share * grid_north)
    return jnp.exp(-0.5 * (scale_east * scale_east + scale_north * scale_north))


def local(state, obs_owner, obs_cell, obs_level, obs_coef, obs_value, obs_error, pattern):
    span_east, span_north, features = state.shape
    tiles_east = lax.axis_size("gx")
    tiles_north = lax.axis_size("gy")
    tiles = tiles_east * tiles_north
    own_tile = lax.axis_index("gx") * tiles_north + lax.axis_index("gy")
    nobs = obs_owner.shape[1]

    west, east = neighbours("gx", state[-2:], state[:2])
    last = jnp.concatenate([west[:, -2:], state[:, -2:], east[:, -2:]], axis=0)
    initial = jnp.concatenate([west[:, :2], state[:, :2], east[:, :2]], axis=0)
    south, north = neighbours("gy", last, initial)

    patterns = lax.all_gather(pattern[0, 0], ("gx", "gy"))
    order, counts = compact(jnp.reshape(own_tile, (1,)).astype(jnp.int32), obs_owner)
    cells = obs_cell.reshape(-1)
    width = -(-tiles // LANES) * LANES
    tables = []
    for batch in range(2):
        blocks = patterns.shape[2]
        rho = distance_weights(
            obs_owner[batch], obs_cell[batch], span_east, span_north, tiles_east, tiles_north
        ).reshape(blocks, nobs // blocks, tiles)
        rho = (rho * patterns[:, batch].T.astype(F32)[:, None, :]).reshape(nobs, tiles)
        columns = jnp.stack(
            [
                obs_coef[batch, 0],
                obs_coef[batch, 1],
                obs_coef[batch, 2],
                obs_level[batch].astype(F32),
                obs_value[batch],
                1.0 / obs_error[batch],
            ],
            axis=1,
        )
        tables.append(
            jnp.concatenate(
                [
                    jnp.pad(columns, ((0, 0), (0, LANES - columns.shape[1]))),
                    jnp.pad(rho, ((0, 0), (0, width - tiles))),
                ],
                axis=1,
            )
        )

    field = forecast(state, west, east, south, north)
    sums = own_sums(0, nobs, tiles, counts, order, cells, field, tables[0])
    first_mix = tile_mix(tiles_east, tiles_north, sums)
    sums = own_sums(1, nobs, tiles, counts, order, cells, field, tables[1], first_mix)
    second_mix = tile_mix(tiles_east, tiles_north, sums)
    return apply_mix(field, first_mix, second_mix).reshape(span_east, span_north, features)


def solution(mesh):
    placed = (P("gx", "gy", None), P(), P(), P(), P(), P(), P(), P("gx", "gy", None, None))
    return jax.shard_map(
        local, mesh=mesh, in_specs=placed, out_specs=P("gx", "gy", None), check_vma=False
    )
```

```python
import functools
import math

import jax
import jax.numpy as jnp
from jax import lax
from jax.experimental import pallas as pl
from jax.experimental.pallas import tpu as pltpu
from jax.sharding import PartitionSpec as P

ENS = 32
LEV = 4
COMP = 3
NSIT = 4
CHUNK = 256
LANES = 128

courant = 0.1
diffusion = 0.08
radius_share = 0.25

VMEM_LIMIT = 48 * 1024 * 1024
HIGHEST = lax.Precision.HIGHEST
F32 = jnp.float32
BF16 = jnp.bfloat16

smem = pl.BlockSpec(memory_space=pltpu.SMEM)
vmem = pl.BlockSpec(memory_space=pltpu.VMEM)


def exact_dot(left, right):
    return jnp.dot(left, right, precision=HIGHEST, preferred_element_type=F32)


def half_dot(left, right):
    return jnp.dot(left, right, preferred_element_type=F32)


def split(values):
    high = values.astype(BF16)
    low = (values - high.astype(F32)).astype(BF16)
    return high, low


def prepare_kernel(tiles_east, tiles_north, pattern_ref, owner_ref, all_ref, list_ref, ranks, held, send_sem, recv_sem):
    tiles = tiles_east * tiles_north
    me = lax.axis_index("gx") * tiles_north + lax.axis_index("gy")

    def device(t):
        return (t // tiles_north, lax.rem(t, tiles_north))

    barrier = pltpu.get_barrier_semaphore()

    def greet(d, carry):
        pl.semaphore_signal(
            barrier, inc=1, device_id=device(lax.rem(me + d, tiles)), device_id_type=pl.DeviceIdType.MESH
        )
        return carry

    lax.fori_loop(1, tiles, greet, 0)
    pl.semaphore_wait(barrier, tiles - 1)

    def send(d, carry):
        pltpu.make_async_remote_copy(
            src_ref=pattern_ref,
            dst_ref=held.at[d - 1],
            send_sem=send_sem,
            recv_sem=recv_sem,
            device_id=device(lax.rem(me + d, tiles)),
            device_id_type=pl.DeviceIdType.MESH,
        ).start()
        return carry

    lax.fori_loop(1, tiles, send, 0)

    rows = owner_ref.shape[0]
    sub = lax.broadcasted_iota(jnp.int32, (LANES, LANES), 0)
    lane = lax.broadcasted_iota(jnp.int32, (LANES, LANES), 1)
    mine = jnp.where(owner_ref[...] == me, 1.0, 0.0)
    before = jnp.where(sub < lane, 1.0, 0.0).astype(BF16)
    ranks[...] = jnp.where(mine > 0.5, half_dot(mine.astype(BF16), before), -1.0)
    place = lax.broadcasted_iota(jnp.int32, (16, LANES), 1).astype(F32).astype(BF16)
    slot = sub.astype(F32)

    def listed(i, carry):
        block = ranks[pl.ds(pl.multiple_of(i * 8, 8), 8), :]
        found = []
        for k in range(8):
            hot = jnp.where(block[k : k + 1] == slot, 1.0, 0.0).astype(BF16)
            found.append(
                lax.dot_general(place, hot, (((1,), (1,)), ((), ())), preferred_element_type=F32)[0:1]
            )
        rows8 = jnp.concatenate(found, axis=0)
        number = jnp.sum(jnp.where(block >= 0.0, 1.0, 0.0), axis=1, keepdims=True)
        list_ref[pl.ds(pl.multiple_of(i * 8, 8), 8), :] = (rows8 + 256.0 * number).astype(jnp.int32)
        return carry

    lax.fori_loop(0, rows // 8, listed, 0)
    all_ref[me] = pattern_ref[...]
    pltpu.make_async_copy(held, held, recv_sem).wait()
    pltpu.make_async_copy(held, held, send_sem).wait()

    def place_one(d, carry):
        all_ref[lax.rem(me - d + tiles, tiles)] = held[d - 1]
        return carry

    lax.fori_loop(1, tiles, place_one, 0)


def prepare(tiles_east, tiles_north, pattern, owners):
    tiles = tiles_east * tiles_north
    flat = pattern.reshape(1, -1).astype(F32)
    flat = jnp.pad(flat, ((0, 0), (0, LANES - flat.shape[1])))
    rows = owners.reshape(-1, LANES)
    return pl.pallas_call(
        functools.partial(prepare_kernel, tiles_east, tiles_north),
        out_shape=(
            jax.ShapeDtypeStruct((tiles, 1, LANES), F32),
            jax.ShapeDtypeStruct(rows.shape, jnp.int32),
        ),
        in_specs=[vmem, vmem],
        out_specs=(vmem, vmem),
        scratch_shapes=[
            pltpu.VMEM(rows.shape, F32),
            pltpu.VMEM((tiles - 1, 1, LANES), F32),
            pltpu.SemaphoreType.DMA,
            pltpu.SemaphoreType.DMA,
        ],
        compiler_params=pltpu.CompilerParams(collective_id=1, has_side_effects=True),
    )(flat, rows)


def forecast_kernel(state_ref, west_ref, east_ref, south_ref, north_ref, out_ref, wide, middle):
    nx, ny, _ = state_ref.shape
    wide[2 : nx + 2, 8 : ny + 8, :] = state_ref[...]
    wide[0:2, 8 : ny + 8, :] = west_ref[...]
    wide[nx + 2 : nx + 4, 8 : ny + 8, :] = east_ref[...]
    wide[:, 6:8, :] = south_ref[...]
    wide[:, ny + 8 : ny + 10, :] = north_ref[...]
    rows = ny + 16

    def updated(src, x, comp, up, um, vp, vm):
        lanes = slice(comp * LANES, (comp + 1) * LANES)
        centre = src[x, :, lanes]
        west = src[x - 1, :, lanes]
        east = src[x + 1, :, lanes]
        south = pltpu.roll(centre, 1, 0)
        north = pltpu.roll(centre, rows - 1, 0)
        flux = up * (centre - west) + um * (east - centre) + vp * (centre - south) + vm * (north - centre)
        return centre - courant * flux + diffusion * ((west + east) + (south + north) - 4.0 * centre)

    def speeds(src, x):
        u = src[x, :, 0:LANES]
        v = src[x, :, LANES : 2 * LANES]
        return jnp.maximum(u, 0.0), jnp.minimum(u, 0.0), jnp.maximum(v, 0.0), jnp.minimum(v, 0.0)

    def first(i, carry):
        parts = speeds(wide, i + 1)
        for comp in range(COMP):
            middle[i, :, comp * LANES : (comp + 1) * LANES] = updated(wide, i + 1, comp, *parts)
        return carry

    lax.fori_loop(0, nx + 2, first, 0)

    def second(i, carry):
        parts = speeds(middle, i + 1)
        for comp in range(COMP):
            new = updated(middle, i + 1, comp, *parts)
            out_ref[pl.ds(pl.multiple_of(i * ny, ny), ny), comp * LANES : (comp + 1) * LANES] = new[8 : ny + 8]
        return carry

    lax.fori_loop(0, nx, second, 0)


def forecast(state, west, east, south, north):
    nx, ny, feat = state.shape
    return pl.pallas_call(
        forecast_kernel,
        out_shape=jax.ShapeDtypeStruct((nx * ny, feat), F32),
        in_specs=[vmem] * 5,
        out_specs=vmem,
        scratch_shapes=[
            pltpu.VMEM((nx + 4, ny + 16, feat), F32),
            pltpu.VMEM((nx + 2, ny + 16, feat), F32),
        ],
        compiler_params=pltpu.CompilerParams(vmem_limit_bytes=VMEM_LIMIT),
    )(state, west, east, south, north)


def sums_kernel(batch, nobs, tiles, mixed, list_ref, cell_ref, field_ref, table_ref, *rest):
    if mixed:
        mix_ref, out_ref, picked, params, total = rest
    else:
        out_ref, picked, params, total = rest
    base = batch * nobs
    blocks = nobs // LANES
    total[...] = jnp.zeros_like(total)
    lane = lax.broadcasted_iota(jnp.int32, (CHUNK, LANES), 1)
    group = lane // ENS
    row = lax.broadcasted_iota(jnp.int32, (CHUNK, 1), 0)
    width = table_ref.shape[1]
    first_lane = 16 + batch * tiles
    tile_of_row = lax.broadcasted_iota(jnp.int32, (width, 256), 0) - first_lane
    tile_of_lane = lax.broadcasted_iota(jnp.int32, (width, 256), 1) // ENS

    def block_of(c, start):
        number = lax.shift_right_logical(list_ref[batch * blocks + c, 0], 8)

        def pick(i, carry):
            for k in range(4):
                j = c * LANES + (list_ref[batch * blocks + c, i * 4 + k] & 255)
                at = start + i * 4 + k
                picked[pl.ds(at, 1), :] = field_ref[pl.ds(cell_ref[base + j], 1), :]
                params[pl.ds(at, 1), :] = table_ref[pl.ds(j, 1), :]
            return carry

        lax.fori_loop(0, lax.shift_right_logical(number + 3, 2), pick, 0)
        return start + number

    count = lax.fori_loop(0, blocks, block_of, 0)

    def chunk(ci, carry):
        rows = pl.ds(pl.multiple_of(ci * CHUNK, CHUNK), CHUNK)
        valid = ci * CHUNK + row < count
        param = jnp.where(valid, params[rows, 0:LANES], 0.0)
        column = batch * 8
        values = (
            param[:, column : column + 1] * picked[rows, 0:LANES]
            + param[:, column + 1 : column + 2] * picked[rows, LANES : 2 * LANES]
            + param[:, column + 2 : column + 3] * picked[rows, 2 * LANES : 3 * LANES]
        )
        values = jnp.where(valid & (group.astype(F32) == param[:, column + 3 : column + 4]), values, 0.0)
        values = values + pltpu.roll(values, 64, 1)
        values = values + pltpu.roll(values, 32, 1)
        if mixed:
            values = exact_dot(values, mix_ref[...])
        centre = jnp.sum(values, axis=1, keepdims=True) / float(LANES)
        inverse_error = param[:, column + 5 : column + 6]
        deviation = (values - centre) * inverse_error
        innovation = (param[:, column + 4 : column + 5] - centre) * inverse_error
        left = jnp.where(group == 0, deviation, jnp.where(lane == ENS, innovation, 0.0))
        high, low = split(left.T[0:48])
        both = jnp.concatenate([high, low], axis=0)
        if width == LANES:
            rho = param
        else:
            rho = jnp.where(valid, params[rows, :], 0.0)
        rho_high, rho_low = split(rho)
        pair = jnp.concatenate([deviation, deviation], axis=1)
        for g in range(tiles // 8):
            spread = jnp.where(tile_of_row == tile_of_lane + g * 8, 1.0, 0.0).astype(BF16)
            weight = half_dot(rho_high, spread) + half_dot(rho_low, spread)
            right_high, right_low = split(weight * pair)
            first = half_dot(both, right_high)
            second = half_dot(high, right_low)
            total[:, g * 256 : (g + 1) * 256] += first[0:48] + first[48:96] + second
        return carry

    lax.fori_loop(0, (count + CHUNK - 1) // CHUNK, chunk, 0)
    small = lax.broadcasted_iota(jnp.int32, (8, LANES), 1) // ENS

    def pack(q, carry):
        lanes = pl.ds(pl.multiple_of(q * LANES, LANES), LANES)
        blocks = [total[8 * r : 8 * r + 8, lanes] for r in range(5)]
        for t in range(4):
            packed = jnp.zeros((8, LANES), F32)
            for r in range(4):
                moved = pltpu.roll(blocks[r], (32 * (r - t)) % LANES, 1) if r != t else blocks[r]
                packed = jnp.where(small == r, moved, packed)
            proj = pltpu.roll(blocks[4], (-32 * t) % LANES, 1) if t else blocks[4]
            out_ref[q * 4 + t, 0:8, :] = packed
            out_ref[q * 4 + t, 8:9, :] = jnp.where(small == 0, proj, 0.0)[0:1]
        return carry

    lax.fori_loop(0, tiles // 4, pack, 0)


def own_sums(batch, nobs, tiles, lists, cells, field, table, mix=None):
    extra = [] if mix is None else [mix]
    return pl.pallas_call(
        functools.partial(sums_kernel, batch, nobs, tiles, mix is not None),
        out_shape=jax.ShapeDtypeStruct((tiles, 9, LANES), F32),
        in_specs=[smem] * 2 + [vmem] * (2 + len(extra)),
        out_specs=vmem,
        scratch_shapes=[
            pltpu.VMEM((nobs + 8, COMP * LANES), F32),
            pltpu.VMEM((nobs + 8, table.shape[1]), F32),
            pltpu.VMEM((48, tiles * ENS), F32),
        ],
        compiler_params=pltpu.CompilerParams(vmem_limit_bytes=VMEM_LIMIT),
    )(lists, cells, field, table, *extra)


def mix_kernel(tiles_east, tiles_north, x_ref, out_ref, held, send_sem, recv_sem):
    tiles = tiles_east * tiles_north
    me = lax.axis_index("gx") * tiles_north + lax.axis_index("gy")

    def device(t):
        return (t // tiles_north, lax.rem(t, tiles_north))

    barrier = pltpu.get_barrier_semaphore()

    def greet(d, carry):
        pl.semaphore_signal(
            barrier, inc=1, device_id=device(lax.rem(me + d, tiles)), device_id_type=pl.DeviceIdType.MESH
        )
        return carry

    lax.fori_loop(1, tiles, greet, 0)
    pl.semaphore_wait(barrier, tiles - 1)

    def send(d, carry):
        target = lax.rem(me + d, tiles)
        pltpu.make_async_remote_copy(
            src_ref=x_ref.at[target],
            dst_ref=held.at[d - 1],
            send_sem=send_sem,
            recv_sem=recv_sem,
            device_id=device(target),
            device_id_type=pl.DeviceIdType.MESH,
        ).start()
        return carry

    lax.fori_loop(1, tiles, send, 0)
    pltpu.make_async_copy(held, held, recv_sem).wait()
    pltpu.make_async_copy(held, held, send_sem).wait()

    total = lax.fori_loop(0, tiles - 1, lambda d, acc: acc + held[d], x_ref[me])
    top = total[0:8]
    cov = jnp.concatenate([top] + [pltpu.roll(top, LANES - 32 * r, 1) for r in range(1, 4)], axis=0)[:, 0:ENS]
    proj = total[8:9, 0:ENS]
    ri = lax.broadcasted_iota(jnp.int32, (ENS, ENS), 0)
    ci = lax.broadcasted_iota(jnp.int32, (ENS, ENS), 1)
    unit = jnp.where(ri == ci, 1.0, 0.0)
    system = (ENS - 1.0) * unit + cov
    bound = jnp.max(jnp.sum(jnp.abs(system), axis=1, keepdims=True), axis=0, keepdims=True)
    approach, root = system / bound, unit
    middle = 1.5 * unit - 0.5 * approach
    approach, root = exact_dot(approach, middle), middle
    for sweep in range(1, NSIT):
        middle = 1.5 * unit - 0.5 * exact_dot(root, approach)
        if sweep < NSIT - 1:
            approach = exact_dot(approach, middle)
        root = exact_dot(middle, root)
    inverse = exact_dot(root, root) / bound
    weights = jnp.sum(inverse * proj, axis=1, keepdims=True)
    shifts = weights + math.sqrt(ENS - 1.0) * root / jnp.sqrt(bound)
    mix = 1.0 / ENS + (shifts - jnp.mean(shifts, axis=0, keepdims=True))
    er = lax.broadcasted_iota(jnp.int32, (ENS, LANES), 0)
    ec = lax.broadcasted_iota(jnp.int32, (ENS, LANES), 1)
    repeated = exact_dot(mix, jnp.where(lax.rem(ec, ENS) == er, 1.0, 0.0))
    full = jnp.concatenate([repeated] * 4, axis=0)
    br = lax.broadcasted_iota(jnp.int32, (LANES, LANES), 0) // ENS
    bc = lax.broadcasted_iota(jnp.int32, (LANES, LANES), 1) // ENS
    out_ref[...] = jnp.where(br == bc, full, 0.0)


def tile_mix(tiles_east, tiles_north, sums):
    tiles = tiles_east * tiles_north
    return pl.pallas_call(
        functools.partial(mix_kernel, tiles_east, tiles_north),
        out_shape=jax.ShapeDtypeStruct((LANES, LANES), F32),
        in_specs=[vmem],
        out_specs=vmem,
        scratch_shapes=[
            pltpu.VMEM((tiles - 1, 9, LANES), F32),
            pltpu.SemaphoreType.DMA,
            pltpu.SemaphoreType.DMA,
        ],
        compiler_params=pltpu.CompilerParams(
            collective_id=0, has_side_effects=True, vmem_limit_bytes=VMEM_LIMIT
        ),
    )(sums)


def apply_kernel(field_ref, one_ref, two_ref, out_ref):
    high, low = split(exact_dot(one_ref[...], two_ref[...]))
    for comp in range(COMP):
        lanes = slice(comp * LANES, (comp + 1) * LANES)
        value_high, value_low = split(field_ref[:, lanes])
        out_ref[:, lanes] = half_dot(value_high, high) + half_dot(value_low, high) + half_dot(value_high, low)


def apply_mix(field, one, two):
    rows, feat = field.shape
    block = 512
    return pl.pallas_call(
        apply_kernel,
        out_shape=jax.ShapeDtypeStruct((rows, feat), F32),
        grid=(rows // block,),
        in_specs=[
            pl.BlockSpec((block, feat), lambda i: (i, 0)),
            pl.BlockSpec((LANES, LANES), lambda i: (0, 0)),
            pl.BlockSpec((LANES, LANES), lambda i: (0, 0)),
        ],
        out_specs=pl.BlockSpec((block, feat), lambda i: (i, 0)),
        compiler_params=pltpu.CompilerParams(vmem_limit_bytes=VMEM_LIMIT),
    )(field, one, two)


def neighbours(axis, last, initial):
    size = lax.axis_size(axis)
    up = [(i, (i + 1) % size) for i in range(size)]
    down = [(j, i) for i, j in up]
    return lax.ppermute(last, axis, up), lax.ppermute(initial, axis, down)


def distance_weights(owners, cells, span_east, span_north, tiles_east, tiles_north):
    grid_east, grid_north = span_east * tiles_east, span_north * tiles_north
    place_east = (owners // tiles_north * span_east + cells // span_north).astype(F32)[:, None]
    place_north = (owners % tiles_north * span_north + cells % span_north).astype(F32)[:, None]
    tile = jnp.arange(tiles_east * tiles_north, dtype=jnp.int32)[None, :]
    centre_east = (tile // tiles_north * span_east).astype(F32) + (span_east - 1) / 2.0
    centre_north = (tile % tiles_north * span_north).astype(F32) + (span_north - 1) / 2.0
    gap_east = place_east - centre_east
    gap_east = jnp.where(gap_east >= grid_east / 2.0, gap_east - grid_east, gap_east)
    gap_east = jnp.where(gap_east < -grid_east / 2.0, gap_east + grid_east, gap_east)
    gap_north = place_north - centre_north
    gap_north = jnp.where(gap_north >= grid_north / 2.0, gap_north - grid_north, gap_north)
    gap_north = jnp.where(gap_north < -grid_north / 2.0, gap_north + grid_north, gap_north)
    scale_east = gap_east / (radius_share * grid_east)
    scale_north = gap_north / (radius_share * grid_north)
    return jnp.exp(-0.5 * (scale_east * scale_east + scale_north * scale_north))


def local(state, obs_owner, obs_cell, obs_level, obs_coef, obs_value, obs_error, pattern):
    span_east, span_north, features = state.shape
    tiles_east = lax.axis_size("gx")
    tiles_north = lax.axis_size("gy")
    tiles = tiles_east * tiles_north
    nobs = obs_owner.shape[1]

    west, east = neighbours("gx", state[-2:], state[:2])
    last = jnp.concatenate([west[:, -2:], state[:, -2:], east[:, -2:]], axis=0)
    initial = jnp.concatenate([west[:, :2], state[:, :2], east[:, :2]], axis=0)
    south, north = neighbours("gy", last, initial)

    patterns, lists = prepare(tiles_east, tiles_north, pattern[0, 0], obs_owner)
    cells = obs_cell.reshape(-1)
    blocks = pattern.shape[3]
    patterns = patterns[:, 0, : 2 * blocks].reshape(tiles, 2, blocks)
    width = -(-(16 + 2 * tiles) // LANES) * LANES
    columns, rhos = [], []
    for batch in range(2):
        rho = distance_weights(
            obs_owner[batch], obs_cell[batch], span_east, span_north, tiles_east, tiles_north
        ).reshape(blocks, nobs // blocks, tiles)
        rhos.append((rho * patterns[:, batch].T[:, None, :]).reshape(nobs, tiles))
        columns += [
            obs_coef[batch],
            obs_level[batch][None].astype(F32),
            obs_value[batch][None],
            1.0 / obs_error[batch][None],
            jnp.zeros((2, nobs), F32),
        ]
    columns = jnp.concatenate(columns, axis=0).T
    spare = jnp.zeros((nobs, width - 16 - 2 * tiles), F32)
    table = jnp.concatenate([columns, *rhos, spare], axis=1)

    field = forecast(state, west, east, south, north)
    sums = own_sums(0, nobs, tiles, lists, cells, field, table)
    first_mix = tile_mix(tiles_east, tiles_north, sums)
    sums = own_sums(1, nobs, tiles, lists, cells, field, table, first_mix)
    second_mix = tile_mix(tiles_east, tiles_north, sums)
    return apply_mix(field, first_mix, second_mix).reshape(span_east, span_north, features)


def solution(mesh):
    placed = (P("gx", "gy", None), P(), P(), P(), P(), P(), P(), P("gx", "gy", None, None))
    return jax.shard_map(
        local, mesh=mesh, in_specs=placed, out_specs=P("gx", "gy", None), check_vma=False
    )
```

```python
import functools
import math

import jax
import jax.numpy as jnp
from jax import lax
from jax.experimental import pallas as pl
from jax.experimental.pallas import tpu as pltpu
from jax.sharding import PartitionSpec as P

ENS = 32
LEV = 4
COMP = 3
NSIT = 4
CHUNK = 256
LANES = 128

courant = 0.1
diffusion = 0.08
radius_share = 0.25

VMEM_LIMIT = 48 * 1024 * 1024
HIGHEST = lax.Precision.HIGHEST
F32 = jnp.float32
BF16 = jnp.bfloat16

smem = pl.BlockSpec(memory_space=pltpu.SMEM)
vmem = pl.BlockSpec(memory_space=pltpu.VMEM)


def exact_dot(left, right):
    return jnp.dot(left, right, precision=HIGHEST, preferred_element_type=F32)


def half_dot(left, right):
    return jnp.dot(left, right, preferred_element_type=F32)


def split(values):
    high = values.astype(BF16)
    low = (values - high.astype(F32)).astype(BF16)
    return high, low


def prepare_kernel(tiles_east, tiles_north, pattern_ref, owner_ref, all_ref, list_ref, ranks, held, send_sem, recv_sem):
    tiles = tiles_east * tiles_north
    me = lax.axis_index("gx") * tiles_north + lax.axis_index("gy")

    def device(t):
        return (t // tiles_north, lax.rem(t, tiles_north))

    barrier = pltpu.get_barrier_semaphore()

    def greet(d, carry):
        pl.semaphore_signal(
            barrier, inc=1, device_id=device(lax.rem(me + d, tiles)), device_id_type=pl.DeviceIdType.MESH
        )
        return carry

    lax.fori_loop(1, tiles, greet, 0)
    pl.semaphore_wait(barrier, tiles - 1)

    def send(d, carry):
        pltpu.make_async_remote_copy(
            src_ref=pattern_ref,
            dst_ref=held.at[d - 1],
            send_sem=send_sem,
            recv_sem=recv_sem,
            device_id=device(lax.rem(me + d, tiles)),
            device_id_type=pl.DeviceIdType.MESH,
        ).start()
        return carry

    lax.fori_loop(1, tiles, send, 0)

    rows = owner_ref.shape[0]
    sub = lax.broadcasted_iota(jnp.int32, (LANES, LANES), 0)
    lane = lax.broadcasted_iota(jnp.int32, (LANES, LANES), 1)
    mine = jnp.where(owner_ref[...] == me, 1.0, 0.0)
    before = jnp.where(sub < lane, 1.0, 0.0).astype(BF16)
    ranks[...] = jnp.where(mine > 0.5, half_dot(mine.astype(BF16), before), -1.0)
    place = lax.broadcasted_iota(jnp.int32, (16, LANES), 1).astype(F32).astype(BF16)
    slot = sub.astype(F32)

    def listed(i, carry):
        block = ranks[pl.ds(pl.multiple_of(i * 8, 8), 8), :]
        found = []
        for k in range(8):
            hot = jnp.where(block[k : k + 1] == slot, 1.0, 0.0).astype(BF16)
            found.append(
                lax.dot_general(place, hot, (((1,), (1,)), ((), ())), preferred_element_type=F32)[0:1]
            )
        rows8 = jnp.concatenate(found, axis=0)
        number = jnp.sum(jnp.where(block >= 0.0, 1.0, 0.0), axis=1, keepdims=True)
        list_ref[pl.ds(pl.multiple_of(i * 8, 8), 8), :] = (rows8 + 256.0 * number).astype(jnp.int32)
        return carry

    lax.fori_loop(0, rows // 8, listed, 0)
    all_ref[me] = pattern_ref[...]
    pltpu.make_async_copy(held, held, recv_sem).wait()
    pltpu.make_async_copy(held, held, send_sem).wait()

    def place_one(d, carry):
        all_ref[lax.rem(me - d + tiles, tiles)] = held[d - 1]
        return carry

    lax.fori_loop(1, tiles, place_one, 0)


def prepare(tiles_east, tiles_north, pattern, owners):
    tiles = tiles_east * tiles_north
    flat = pattern.reshape(1, -1).astype(F32)
    flat = jnp.pad(flat, ((0, 0), (0, LANES - flat.shape[1])))
    rows = owners.reshape(-1, LANES)
    return pl.pallas_call(
        functools.partial(prepare_kernel, tiles_east, tiles_north),
        out_shape=(
            jax.ShapeDtypeStruct((tiles, 1, LANES), F32),
            jax.ShapeDtypeStruct(rows.shape, jnp.int32),
        ),
        in_specs=[vmem, vmem],
        out_specs=(vmem, vmem),
        scratch_shapes=[
            pltpu.VMEM(rows.shape, F32),
            pltpu.VMEM((tiles - 1, 1, LANES), F32),
            pltpu.SemaphoreType.DMA,
            pltpu.SemaphoreType.DMA,
        ],
        compiler_params=pltpu.CompilerParams(collective_id=1, has_side_effects=True),
    )(flat, rows)


def forecast_kernel(state_ref, west_ref, east_ref, south_ref, north_ref, out_ref, wide, middle):
    nx, ny, _ = state_ref.shape
    wide[2 : nx + 2, 8 : ny + 8, :] = state_ref[...]
    wide[0:2, 8 : ny + 8, :] = west_ref[...]
    wide[nx + 2 : nx + 4, 8 : ny + 8, :] = east_ref[...]
    wide[:, 6:8, :] = south_ref[...]
    wide[:, ny + 8 : ny + 10, :] = north_ref[...]
    rows = ny + 16

    def updated(src, x, comp, up, um, vp, vm):
        lanes = slice(comp * LANES, (comp + 1) * LANES)
        centre = src[x, :, lanes]
        west = src[x - 1, :, lanes]
        east = src[x + 1, :, lanes]
        south = pltpu.roll(centre, 1, 0)
        north = pltpu.roll(centre, rows - 1, 0)
        flux = up * (centre - west) + um * (east - centre) + vp * (centre - south) + vm * (north - centre)
        return centre - courant * flux + diffusion * ((west + east) + (south + north) - 4.0 * centre)

    def speeds(src, x):
        u = src[x, :, 0:LANES]
        v = src[x, :, LANES : 2 * LANES]
        return jnp.maximum(u, 0.0), jnp.minimum(u, 0.0), jnp.maximum(v, 0.0), jnp.minimum(v, 0.0)

    def first(i, carry):
        parts = speeds(wide, i + 1)
        for comp in range(COMP):
            middle[i, :, comp * LANES : (comp + 1) * LANES] = updated(wide, i + 1, comp, *parts)
        return carry

    lax.fori_loop(0, nx + 2, first, 0)

    def second(i, carry):
        parts = speeds(middle, i + 1)
        for comp in range(COMP):
            new = updated(middle, i + 1, comp, *parts)
            out_ref[pl.ds(pl.multiple_of(i * ny, ny), ny), comp * LANES : (comp + 1) * LANES] = new[8 : ny + 8]
        return carry

    lax.fori_loop(0, nx, second, 0)


def forecast(state, west, east, south, north):
    nx, ny, feat = state.shape
    return pl.pallas_call(
        forecast_kernel,
        out_shape=jax.ShapeDtypeStruct((nx * ny, feat), F32),
        in_specs=[vmem] * 5,
        out_specs=vmem,
        scratch_shapes=[
            pltpu.VMEM((nx + 4, ny + 16, feat), F32),
            pltpu.VMEM((nx + 2, ny + 16, feat), F32),
        ],
        compiler_params=pltpu.CompilerParams(vmem_limit_bytes=VMEM_LIMIT),
    )(state, west, east, south, north)


def sums_kernel(batch, nobs, tiles, mixed, list_ref, cell_ref, field_ref, table_ref, *rest):
    if mixed:
        mix_ref, out_ref, picked, params, total = rest
    else:
        out_ref, picked, params, total = rest
    base = batch * nobs
    blocks = nobs // LANES
    total[...] = jnp.zeros_like(total)
    lane = lax.broadcasted_iota(jnp.int32, (CHUNK, LANES), 1)
    group = lane // ENS
    row = lax.broadcasted_iota(jnp.int32, (CHUNK, 1), 0)
    width = table_ref.shape[1]
    first_lane = 16 + batch * tiles
    tile_of_row = lax.broadcasted_iota(jnp.int32, (width, 256), 0) - first_lane
    tile_of_lane = lax.broadcasted_iota(jnp.int32, (width, 256), 1) // ENS

    def block_of(c, start):
        number = lax.shift_right_logical(list_ref[batch * blocks + c, 0], 8)

        def pick(i, carry):
            js = [c * LANES + (list_ref[batch * blocks + c, i * 8 + k] & 255) for k in range(8)]
            values = [field_ref[pl.ds(cell_ref[base + j], 1), :] for j in js]
            entries = [table_ref[pl.ds(j, 1), :] for j in js]
            for k in range(8):
                picked[pl.ds(start + i * 8 + k, 1), :] = values[k]
                params[pl.ds(start + i * 8 + k, 1), :] = entries[k]
            return carry

        lax.fori_loop(0, lax.shift_right_logical(number + 7, 3), pick, 0)
        return start + number

    count = lax.fori_loop(0, blocks, block_of, 0)

    def chunk(ci, carry):
        rows = pl.ds(pl.multiple_of(ci * CHUNK, CHUNK), CHUNK)
        valid = ci * CHUNK + row < count
        param = jnp.where(valid, params[rows, 0:LANES], 0.0)
        column = batch * 8
        values = (
            param[:, column : column + 1] * picked[rows, 0:LANES]
            + param[:, column + 1 : column + 2] * picked[rows, LANES : 2 * LANES]
            + param[:, column + 2 : column + 3] * picked[rows, 2 * LANES : 3 * LANES]
        )
        values = jnp.where(valid & (group.astype(F32) == param[:, column + 3 : column + 4]), values, 0.0)
        values = values + pltpu.roll(values, 64, 1)
        values = values + pltpu.roll(values, 32, 1)
        if mixed:
            values = exact_dot(values, mix_ref[...])
        centre = jnp.sum(values, axis=1, keepdims=True) / float(LANES)
        inverse_error = param[:, column + 5 : column + 6]
        deviation = (values - centre) * inverse_error
        innovation = (param[:, column + 4 : column + 5] - centre) * inverse_error
        left = jnp.where(group == 0, deviation, jnp.where(lane == ENS, innovation, 0.0))
        high, low = split(left.T[0:48])
        both = jnp.concatenate([high, low], axis=0)
        if width == LANES:
            rho = param
        else:
            rho = jnp.where(valid, params[rows, :], 0.0)
        rho_both = jnp.concatenate(split(rho), axis=1)
        pair = jnp.concatenate([deviation, deviation], axis=1)
        for g in range(tiles // 8):
            spread = jnp.where(tile_of_row == tile_of_lane + g * 8, 1.0, 0.0).astype(BF16)
            weight = half_dot(rho_both, jnp.concatenate([spread, spread], axis=0))
            right_high, right_low = split(weight * pair)
            first = half_dot(both, right_high)
            second = half_dot(high, right_low)
            total[:, g * 256 : (g + 1) * 256] += first[0:48] + first[48:96] + second
        return carry

    lax.fori_loop(0, (count + CHUNK - 1) // CHUNK, chunk, 0)
    small = lax.broadcasted_iota(jnp.int32, (8, LANES), 1) // ENS

    def pack(q, carry):
        lanes = pl.ds(pl.multiple_of(q * LANES, LANES), LANES)
        blocks = [total[8 * r : 8 * r + 8, lanes] for r in range(5)]
        for t in range(4):
            packed = jnp.zeros((8, LANES), F32)
            for r in range(4):
                moved = pltpu.roll(blocks[r], (32 * (r - t)) % LANES, 1) if r != t else blocks[r]
                packed = jnp.where(small == r, moved, packed)
            proj = pltpu.roll(blocks[4], (-32 * t) % LANES, 1) if t else blocks[4]
            out_ref[q * 4 + t, 0:8, :] = packed
            out_ref[q * 4 + t, 8:9, :] = jnp.where(small == 0, proj, 0.0)[0:1]
        return carry

    lax.fori_loop(0, tiles // 4, pack, 0)


def own_sums(batch, nobs, tiles, lists, cells, field, table, mix=None):
    extra = [] if mix is None else [mix]
    return pl.pallas_call(
        functools.partial(sums_kernel, batch, nobs, tiles, mix is not None),
        out_shape=jax.ShapeDtypeStruct((tiles, 9, LANES), F32),
        in_specs=[smem] * 2 + [vmem] * (2 + len(extra)),
        out_specs=vmem,
        scratch_shapes=[
            pltpu.VMEM((nobs + 8, COMP * LANES), F32),
            pltpu.VMEM((nobs + 8, table.shape[1]), F32),
            pltpu.VMEM((48, tiles * ENS), F32),
        ],
        compiler_params=pltpu.CompilerParams(vmem_limit_bytes=VMEM_LIMIT),
    )(lists, cells, field, table, *extra)


def mix_kernel(tiles_east, tiles_north, x_ref, out_ref, held, send_sem, recv_sem):
    tiles = tiles_east * tiles_north
    me = lax.axis_index("gx") * tiles_north + lax.axis_index("gy")

    def device(t):
        return (t // tiles_north, lax.rem(t, tiles_north))

    barrier = pltpu.get_barrier_semaphore()

    def greet(d, carry):
        pl.semaphore_signal(
            barrier, inc=1, device_id=device(lax.rem(me + d, tiles)), device_id_type=pl.DeviceIdType.MESH
        )
        return carry

    lax.fori_loop(1, tiles, greet, 0)
    pl.semaphore_wait(barrier, tiles - 1)

    def send(d, carry):
        target = lax.rem(me + d, tiles)
        pltpu.make_async_remote_copy(
            src_ref=x_ref.at[target],
            dst_ref=held.at[d - 1],
            send_sem=send_sem,
            recv_sem=recv_sem,
            device_id=device(target),
            device_id_type=pl.DeviceIdType.MESH,
        ).start()
        return carry

    lax.fori_loop(1, tiles, send, 0)
    pltpu.make_async_copy(held, held, recv_sem).wait()
    pltpu.make_async_copy(held, held, send_sem).wait()

    total = lax.fori_loop(0, tiles - 1, lambda d, acc: acc + held[d], x_ref[me])
    top = total[0:8]
    cov = jnp.concatenate([top] + [pltpu.roll(top, LANES - 32 * r, 1) for r in range(1, 4)], axis=0)[:, 0:ENS]
    proj = total[8:9, 0:ENS]
    ri = lax.broadcasted_iota(jnp.int32, (ENS, ENS), 0)
    ci = lax.broadcasted_iota(jnp.int32, (ENS, ENS), 1)
    unit = jnp.where(ri == ci, 1.0, 0.0)
    system = (ENS - 1.0) * unit + cov
    bound = jnp.max(jnp.sum(jnp.abs(system), axis=1, keepdims=True), axis=0, keepdims=True)
    approach, root = system / bound, unit
    middle = 1.5 * unit - 0.5 * approach
    approach, root = exact_dot(approach, middle), middle
    for sweep in range(1, NSIT):
        middle = 1.5 * unit - 0.5 * exact_dot(root, approach)
        if sweep < NSIT - 1:
            approach = exact_dot(approach, middle)
        root = exact_dot(middle, root)
    inverse = exact_dot(root, root) / bound
    weights = jnp.sum(inverse * proj, axis=1, keepdims=True)
    shifts = weights + math.sqrt(ENS - 1.0) * root / jnp.sqrt(bound)
    mix = 1.0 / ENS + (shifts - jnp.mean(shifts, axis=0, keepdims=True))
    er = lax.broadcasted_iota(jnp.int32, (ENS, LANES), 0)
    ec = lax.broadcasted_iota(jnp.int32, (ENS, LANES), 1)
    repeated = exact_dot(mix, jnp.where(lax.rem(ec, ENS) == er, 1.0, 0.0))
    full = jnp.concatenate([repeated] * 4, axis=0)
    br = lax.broadcasted_iota(jnp.int32, (LANES, LANES), 0) // ENS
    bc = lax.broadcasted_iota(jnp.int32, (LANES, LANES), 1) // ENS
    out_ref[...] = jnp.where(br == bc, full, 0.0)


def tile_mix(tiles_east, tiles_north, sums):
    tiles = tiles_east * tiles_north
    return pl.pallas_call(
        functools.partial(mix_kernel, tiles_east, tiles_north),
        out_shape=jax.ShapeDtypeStruct((LANES, LANES), F32),
        in_specs=[vmem],
        out_specs=vmem,
        scratch_shapes=[
            pltpu.VMEM((tiles - 1, 9, LANES), F32),
            pltpu.SemaphoreType.DMA,
            pltpu.SemaphoreType.DMA,
        ],
        compiler_params=pltpu.CompilerParams(
            collective_id=0, has_side_effects=True, vmem_limit_bytes=VMEM_LIMIT
        ),
    )(sums)


def apply_kernel(field_ref, one_ref, two_ref, out_ref):
    high, low = split(exact_dot(one_ref[...], two_ref[...]))
    for comp in range(COMP):
        lanes = slice(comp * LANES, (comp + 1) * LANES)
        value_high, value_low = split(field_ref[:, lanes])
        out_ref[:, lanes] = half_dot(value_high, high) + half_dot(value_low, high) + half_dot(value_high, low)


def apply_mix(field, one, two):
    rows, feat = field.shape
    block = 512
    return pl.pallas_call(
        apply_kernel,
        out_shape=jax.ShapeDtypeStruct((rows, feat), F32),
        grid=(rows // block,),
        in_specs=[
            pl.BlockSpec((block, feat), lambda i: (i, 0)),
            pl.BlockSpec((LANES, LANES), lambda i: (0, 0)),
            pl.BlockSpec((LANES, LANES), lambda i: (0, 0)),
        ],
        out_specs=pl.BlockSpec((block, feat), lambda i: (i, 0)),
        compiler_params=pltpu.CompilerParams(vmem_limit_bytes=VMEM_LIMIT),
    )(field, one, two)


def neighbours(axis, last, initial):
    size = lax.axis_size(axis)
    up = [(i, (i + 1) % size) for i in range(size)]
    down = [(j, i) for i, j in up]
    return lax.ppermute(last, axis, up), lax.ppermute(initial, axis, down)


def table_kernel(
    nx, ny, tiles_east, tiles_north, blocks,
    owner_ref, cell_ref, level_ref, coef_ref, value_ref, error_ref, pattern_ref, out_ref,
):
    tiles = tiles_east * tiles_north
    nobs = owner_ref.shape[1]
    width = out_ref.shape[1]
    grid_east, grid_north = float(nx * tiles_east), float(ny * tiles_north)

    def parts(value, size):
        whole = jnp.floor((value + 0.5) * (1.0 / size))
        return whole, value - whole * size

    tile = lax.broadcasted_iota(jnp.int32, (tiles, LANES), 0).astype(F32)
    tile_east, tile_north = parts(tile, tiles_north)
    centre_east = tile_east * nx + (nx - 1) / 2.0
    centre_north = tile_north * ny + (ny - 1) / 2.0
    lane = lax.broadcasted_iota(jnp.int32, (tiles, LANES), 1)

    def scaled(place, centre, grid):
        gap = place - centre
        gap = jnp.where(gap >= grid / 2.0, gap - grid, gap)
        gap = jnp.where(gap < -grid / 2.0, gap + grid, gap)
        return gap * (1.0 / (radius_share * grid))

    def one(c, carry):
        at = pl.ds(pl.multiple_of(c * LANES, LANES), LANES)
        columns, rhos = [], []
        for batch in range(2):
            row = slice(batch, batch + 1)
            owner_east, owner_north = parts(owner_ref[row, at].astype(F32), tiles_north)
            cell_east, cell_north = parts(cell_ref[row, at].astype(F32), ny)
            far_east = scaled(owner_east * nx + cell_east, centre_east, grid_east)
            far_north = scaled(owner_north * ny + cell_north, centre_north, grid_north)
            used = batch * blocks + (c * LANES) // (nobs // blocks)
            mask = jnp.sum(jnp.where(lane == used, pattern_ref[...], 0.0), axis=1, keepdims=True)
            rhos.append(mask * jnp.exp(-0.5 * (far_east * far_east + far_north * far_north)))
            columns += [
                coef_ref[3 * batch : 3 * batch + 3, at],
                level_ref[row, at].astype(F32),
                value_ref[row, at],
                1.0 / error_ref[row, at],
                jnp.zeros((2, LANES), F32),
            ]
        spare = jnp.zeros((width - 16 - 2 * tiles, LANES), F32)
        out_ref[at, :] = jnp.concatenate([*columns, *rhos, spare], axis=0).T
        return carry

    lax.fori_loop(0, nobs // LANES, one, 0)


def make_table(nx, ny, tiles_east, tiles_north, blocks, patterns, owner, cell, level, coef, value, error):
    tiles = tiles_east * tiles_north
    nobs = owner.shape[1]
    width = -(-(16 + 2 * tiles) // LANES) * LANES
    return pl.pallas_call(
        functools.partial(table_kernel, nx, ny, tiles_east, tiles_north, blocks),
        out_shape=jax.ShapeDtypeStruct((nobs, width), F32),
        in_specs=[vmem] * 7,
        out_specs=vmem,
        compiler_params=pltpu.CompilerParams(vmem_limit_bytes=VMEM_LIMIT),
        cost_estimate=pl.CostEstimate(flops=50_000_000, bytes_accessed=12_000_000, transcendentals=0),
    )(owner, cell, level, coef.reshape(6, nobs), value, error, patterns.reshape(tiles, LANES))


def local(state, obs_owner, obs_cell, obs_level, obs_coef, obs_value, obs_error, pattern):
    span_east, span_north, features = state.shape
    tiles_east = lax.axis_size("gx")
    tiles_north = lax.axis_size("gy")
    tiles = tiles_east * tiles_north
    nobs = obs_owner.shape[1]

    west, east = neighbours("gx", state[-2:], state[:2])
    patterns, lists = prepare(tiles_east, tiles_north, pattern[0, 0], obs_owner)
    last = jnp.concatenate([west[:, -2:], state[:, -2:], east[:, -2:]], axis=0)
    initial = jnp.concatenate([west[:, :2], state[:, :2], east[:, :2]], axis=0)
    last, initial, patterns = lax.optimization_barrier((last, initial, patterns))
    south, north = neighbours("gy", last, initial)
    cells = obs_cell.reshape(-1)
    table = make_table(
        span_east, span_north, tiles_east, tiles_north, pattern.shape[3], patterns,
        obs_owner, obs_cell, obs_level, obs_coef, obs_value, obs_error,
    )

    field = forecast(state, west, east, south, north)
    sums = own_sums(0, nobs, tiles, lists, cells, field, table)
    first_mix = tile_mix(tiles_east, tiles_north, sums)
    sums = own_sums(1, nobs, tiles, lists, cells, field, table, first_mix)
    second_mix = tile_mix(tiles_east, tiles_north, sums)
    return apply_mix(field, first_mix, second_mix).reshape(span_east, span_north, features)


def solution(mesh):
    placed = (P("gx", "gy", None), P(), P(), P(), P(), P(), P(), P("gx", "gy", None, None))
    return jax.shard_map(
        local, mesh=mesh, in_specs=placed, out_specs=P("gx", "gy", None), check_vma=False
    )
```

```python
import functools
import math

import jax
import jax.numpy as jnp
from jax import lax
from jax.experimental import pallas as pl
from jax.experimental.pallas import tpu as pltpu
from jax.sharding import PartitionSpec as P

ENS = 32
LEV = 4
COMP = 3
NSIT = 4
CHUNK = 256
LANES = 128

courant = 0.1
diffusion = 0.08
radius_share = 0.25

VMEM_LIMIT = 48 * 1024 * 1024
HIGHEST = lax.Precision.HIGHEST
F32 = jnp.float32
BF16 = jnp.bfloat16

smem = pl.BlockSpec(memory_space=pltpu.SMEM)
vmem = pl.BlockSpec(memory_space=pltpu.VMEM)


def exact_dot(left, right):
    return jnp.dot(left, right, precision=HIGHEST, preferred_element_type=F32)


def half_dot(left, right):
    return jnp.dot(left, right, preferred_element_type=F32)


def split(values):
    high = values.astype(BF16)
    low = (values - high.astype(F32)).astype(BF16)
    return high, low


def prepare_kernel(tiles_east, tiles_north, pattern_ref, owner_ref, all_ref, list_ref, raw, ranks, held, send_sem, recv_sem):
    tiles = tiles_east * tiles_north
    me = lax.axis_index("gx") * tiles_north + lax.axis_index("gy")

    def device(t):
        return (t // tiles_north, lax.rem(t, tiles_north))

    barrier = pltpu.get_barrier_semaphore()

    def greet(d, carry):
        pl.semaphore_signal(
            barrier, inc=1, device_id=device(lax.rem(me + d, tiles)), device_id_type=pl.DeviceIdType.MESH
        )
        return carry

    lax.fori_loop(1, tiles, greet, 0)
    groups = owner_ref.shape[1] // LANES
    for c in range(groups):
        for batch in range(2):
            raw[batch * groups + c : batch * groups + c + 1, :] = owner_ref[
                batch : batch + 1, c * LANES : (c + 1) * LANES
            ]
    pl.semaphore_wait(barrier, tiles - 1)

    def send(d, carry):
        pltpu.make_async_remote_copy(
            src_ref=pattern_ref,
            dst_ref=held.at[d - 1],
            send_sem=send_sem,
            recv_sem=recv_sem,
            device_id=device(lax.rem(me + d, tiles)),
            device_id_type=pl.DeviceIdType.MESH,
        ).start()
        return carry

    lax.fori_loop(1, tiles, send, 0)

    rows = list_ref.shape[0]
    sub = lax.broadcasted_iota(jnp.int32, (LANES, LANES), 0)
    lane = lax.broadcasted_iota(jnp.int32, (LANES, LANES), 1)
    mine = jnp.where(raw[...] == me, 1.0, 0.0)
    before = jnp.where(sub < lane, 1.0, 0.0).astype(BF16)
    ranks[...] = jnp.where(mine > 0.5, half_dot(mine.astype(BF16), before), -1.0)
    place = lax.broadcasted_iota(jnp.int32, (16, LANES), 1).astype(F32).astype(BF16)
    slot = sub.astype(F32)

    def listed(i, carry):
        block = ranks[pl.ds(pl.multiple_of(i * 8, 8), 8), :]
        found = []
        for k in range(8):
            hot = jnp.where(block[k : k + 1] == slot, 1.0, 0.0).astype(BF16)
            found.append(
                lax.dot_general(place, hot, (((1,), (1,)), ((), ())), preferred_element_type=F32)[0:1]
            )
        rows8 = jnp.concatenate(found, axis=0)
        number = jnp.sum(jnp.where(block >= 0.0, 1.0, 0.0), axis=1, keepdims=True)
        list_ref[pl.ds(pl.multiple_of(i * 8, 8), 8), :] = (rows8 + 256.0 * number).astype(jnp.int32)
        return carry

    lax.fori_loop(0, rows // 8, listed, 0)
    all_ref[me] = pattern_ref[...]
    pltpu.make_async_copy(held, held, recv_sem).wait()
    pltpu.make_async_copy(held, held, send_sem).wait()

    def place_one(d, carry):
        all_ref[lax.rem(me - d + tiles, tiles)] = held[d - 1]
        return carry

    lax.fori_loop(1, tiles, place_one, 0)


def prepare(tiles_east, tiles_north, pattern, owners):
    tiles = tiles_east * tiles_north
    flat = pattern.reshape(1, -1).astype(F32)
    flat = jnp.pad(flat, ((0, 0), (0, LANES - flat.shape[1])))
    rows = (owners.size // LANES, LANES)
    return pl.pallas_call(
        functools.partial(prepare_kernel, tiles_east, tiles_north),
        out_shape=(
            jax.ShapeDtypeStruct((tiles, 1, LANES), F32),
            jax.ShapeDtypeStruct(rows, jnp.int32),
        ),
        in_specs=[vmem, vmem],
        out_specs=(vmem, vmem),
        scratch_shapes=[
            pltpu.VMEM(rows, jnp.int32),
            pltpu.VMEM(rows, F32),
            pltpu.VMEM((tiles - 1, 1, LANES), F32),
            pltpu.SemaphoreType.DMA,
            pltpu.SemaphoreType.DMA,
        ],
        compiler_params=pltpu.CompilerParams(collective_id=1, has_side_effects=True),
    )(flat, owners)


def forecast_kernel(state_ref, west_ref, east_ref, south_ref, north_ref, out_ref, wide, middle):
    nx, ny, _ = state_ref.shape
    wide[2 : nx + 2, 8 : ny + 8, :] = state_ref[...]
    wide[0:2, 8 : ny + 8, :] = west_ref[...]
    wide[nx + 2 : nx + 4, 8 : ny + 8, :] = east_ref[...]
    wide[:, 6:8, :] = south_ref[...]
    wide[:, ny + 8 : ny + 10, :] = north_ref[...]
    rows = ny + 16

    def updated(src, x, comp, up, um, vp, vm):
        lanes = slice(comp * LANES, (comp + 1) * LANES)
        centre = src[x, :, lanes]
        west = src[x - 1, :, lanes]
        east = src[x + 1, :, lanes]
        south = pltpu.roll(centre, 1, 0)
        north = pltpu.roll(centre, rows - 1, 0)
        flux = up * (centre - west) + um * (east - centre) + vp * (centre - south) + vm * (north - centre)
        return centre - courant * flux + diffusion * ((west + east) + (south + north) - 4.0 * centre)

    def speeds(src, x):
        u = src[x, :, 0:LANES]
        v = src[x, :, LANES : 2 * LANES]
        return jnp.maximum(u, 0.0), jnp.minimum(u, 0.0), jnp.maximum(v, 0.0), jnp.minimum(v, 0.0)

    def first(i, carry):
        parts = speeds(wide, i + 1)
        for comp in range(COMP):
            middle[i, :, comp * LANES : (comp + 1) * LANES] = updated(wide, i + 1, comp, *parts)
        return carry

    lax.fori_loop(0, nx + 2, first, 0)

    def second(i, carry):
        parts = speeds(middle, i + 1)
        for comp in range(COMP):
            new = updated(middle, i + 1, comp, *parts)
            out_ref[pl.ds(pl.multiple_of(i * ny, ny), ny), comp * LANES : (comp + 1) * LANES] = new[8 : ny + 8]
        return carry

    lax.fori_loop(0, nx, second, 0)


def forecast(state, west, east, south, north):
    nx, ny, feat = state.shape
    return pl.pallas_call(
        forecast_kernel,
        out_shape=jax.ShapeDtypeStruct((nx * ny, feat), F32),
        in_specs=[vmem] * 5,
        out_specs=vmem,
        scratch_shapes=[
            pltpu.VMEM((nx + 4, ny + 16, feat), F32),
            pltpu.VMEM((nx + 2, ny + 16, feat), F32),
        ],
        compiler_params=pltpu.CompilerParams(vmem_limit_bytes=VMEM_LIMIT),
    )(state, west, east, south, north)


def sums_kernel(batch, nobs, tiles, mixed, list_ref, cell_ref, field_ref, table_ref, *rest):
    if mixed:
        mix_ref, out_ref, picked, params, total = rest
    else:
        out_ref, picked, params, total = rest
    blocks = nobs // LANES
    total[...] = jnp.zeros_like(total)
    lane = lax.broadcasted_iota(jnp.int32, (CHUNK, LANES), 1)
    group = lane // ENS
    row = lax.broadcasted_iota(jnp.int32, (CHUNK, 1), 0)
    first_lane = 16 + batch * tiles

    def block_of(c, start):
        number = lax.shift_right_logical(list_ref[batch * blocks + c, 0], 8)

        def pick(i, carry):
            js = [c * LANES + (list_ref[batch * blocks + c, i * 8 + k] & 255) for k in range(8)]
            values = [field_ref[pl.ds(cell_ref[batch, j], 1), :] for j in js]
            entries = [table_ref[pl.ds(j, 1), :] for j in js]
            for k in range(8):
                picked[pl.ds(start + i * 8 + k, 1), :] = values[k]
                params[pl.ds(start + i * 8 + k, 1), :] = entries[k]
            return carry

        lax.fori_loop(0, lax.shift_right_logical(number + 7, 3), pick, 0)
        return start + number

    count = lax.fori_loop(0, blocks, block_of, 0)

    def chunk(ci, carry):
        rows = pl.ds(pl.multiple_of(ci * CHUNK, CHUNK), CHUNK)
        valid = ci * CHUNK + row < count
        param = jnp.where(valid, params[rows, 0:LANES], 0.0)
        column = batch * 8
        values = (
            param[:, column : column + 1] * picked[rows, 0:LANES]
            + param[:, column + 1 : column + 2] * picked[rows, LANES : 2 * LANES]
            + param[:, column + 2 : column + 3] * picked[rows, 2 * LANES : 3 * LANES]
        )
        values = jnp.where(valid & (group.astype(F32) == param[:, column + 3 : column + 4]), values, 0.0)
        values = values + pltpu.roll(values, 64, 1)
        values = values + pltpu.roll(values, 32, 1)
        if mixed:
            values = exact_dot(values, mix_ref[...])
        centre = jnp.sum(values, axis=1, keepdims=True) / float(LANES)
        inverse_error = param[:, column + 5 : column + 6]
        deviation = (values - centre) * inverse_error
        innovation = (param[:, column + 4 : column + 5] - centre) * inverse_error
        left = jnp.where(group == 0, deviation, jnp.where(lane == ENS, innovation, 0.0))
        high, low = split(left.T[0:48])
        both = jnp.concatenate([high, low], axis=0)
        pair = jnp.concatenate([deviation, deviation], axis=1)
        for g in range(tiles // 8):
            spread = []
            for h in range(2):
                column = first_lane + g * 8 + h * 4
                whole, inside = column // LANES, column % LANES
                source = param if whole == 0 else jnp.where(
                    valid, params[rows, whole * LANES : (whole + 1) * LANES], 0.0
                )
                spread.append(jnp.take_along_axis(source, group + inside, axis=1, mode="promise_in_bounds"))
            weight = jnp.concatenate(spread, axis=1)
            right_high, right_low = split(weight * pair)
            first = half_dot(both, right_high)
            second = half_dot(high, right_low)
            total[:, g * 256 : (g + 1) * 256] += first[0:48] + first[48:96] + second
        return carry

    lax.fori_loop(0, (count + CHUNK - 1) // CHUNK, chunk, 0)
    small = lax.broadcasted_iota(jnp.int32, (8, LANES), 1) // ENS

    def pack(q, carry):
        lanes = pl.ds(pl.multiple_of(q * LANES, LANES), LANES)
        blocks = [total[8 * r : 8 * r + 8, lanes] for r in range(5)]
        for t in range(4):
            packed = jnp.zeros((8, LANES), F32)
            for r in range(4):
                moved = pltpu.roll(blocks[r], (32 * (r - t)) % LANES, 1) if r != t else blocks[r]
                packed = jnp.where(small == r, moved, packed)
            proj = pltpu.roll(blocks[4], (-32 * t) % LANES, 1) if t else blocks[4]
            out_ref[q * 4 + t, 0:8, :] = packed
            out_ref[q * 4 + t, 8:9, :] = jnp.where(small == 0, proj, 0.0)[0:1]
        return carry

    lax.fori_loop(0, tiles // 4, pack, 0)


def own_sums(batch, nobs, tiles, lists, cells, field, table, mix=None):
    extra = [] if mix is None else [mix]
    return pl.pallas_call(
        functools.partial(sums_kernel, batch, nobs, tiles, mix is not None),
        out_shape=jax.ShapeDtypeStruct((tiles, 9, LANES), F32),
        in_specs=[smem] * 2 + [vmem] * (2 + len(extra)),
        out_specs=vmem,
        scratch_shapes=[
            pltpu.VMEM((nobs + 8, COMP * LANES), F32),
            pltpu.VMEM((nobs + 8, table.shape[1]), F32),
            pltpu.VMEM((48, tiles * ENS), F32),
        ],
        compiler_params=pltpu.CompilerParams(vmem_limit_bytes=VMEM_LIMIT),
    )(lists, cells, field, table, *extra)


def mix_kernel(tiles_east, tiles_north, x_ref, out_ref, held, send_sem, recv_sem):
    tiles = tiles_east * tiles_north
    me = lax.axis_index("gx") * tiles_north + lax.axis_index("gy")

    def device(t):
        return (t // tiles_north, lax.rem(t, tiles_north))

    barrier = pltpu.get_barrier_semaphore()

    def greet(d, carry):
        pl.semaphore_signal(
            barrier, inc=1, device_id=device(lax.rem(me + d, tiles)), device_id_type=pl.DeviceIdType.MESH
        )
        return carry

    lax.fori_loop(1, tiles, greet, 0)
    pl.semaphore_wait(barrier, tiles - 1)

    def send(d, carry):
        target = lax.rem(me + d, tiles)
        pltpu.make_async_remote_copy(
            src_ref=x_ref.at[target],
            dst_ref=held.at[d - 1],
            send_sem=send_sem,
            recv_sem=recv_sem,
            device_id=device(target),
            device_id_type=pl.DeviceIdType.MESH,
        ).start()
        return carry

    lax.fori_loop(1, tiles, send, 0)
    pltpu.make_async_copy(held, held, recv_sem).wait()
    pltpu.make_async_copy(held, held, send_sem).wait()

    total = lax.fori_loop(0, tiles - 1, lambda d, acc: acc + held[d], x_ref[me])
    top = total[0:8]
    cov = jnp.concatenate([top] + [pltpu.roll(top, LANES - 32 * r, 1) for r in range(1, 4)], axis=0)[:, 0:ENS]
    proj = total[8:9, 0:ENS]
    ri = lax.broadcasted_iota(jnp.int32, (ENS, ENS), 0)
    ci = lax.broadcasted_iota(jnp.int32, (ENS, ENS), 1)
    unit = jnp.where(ri == ci, 1.0, 0.0)
    system = (ENS - 1.0) * unit + cov
    bound = jnp.max(jnp.sum(jnp.abs(system), axis=1, keepdims=True), axis=0, keepdims=True)
    approach, root = system / bound, unit
    middle = 1.5 * unit - 0.5 * approach
    approach, root = exact_dot(approach, middle), middle
    for sweep in range(1, NSIT):
        middle = 1.5 * unit - 0.5 * exact_dot(root, approach)
        if sweep < NSIT - 1:
            approach = exact_dot(approach, middle)
        root = exact_dot(middle, root)
    inverse = exact_dot(root, root) / bound
    weights = jnp.sum(inverse * proj, axis=1, keepdims=True)
    shifts = weights + math.sqrt(ENS - 1.0) * root / jnp.sqrt(bound)
    mix = 1.0 / ENS + (shifts - jnp.mean(shifts, axis=0, keepdims=True))
    er = lax.broadcasted_iota(jnp.int32, (ENS, LANES), 0)
    ec = lax.broadcasted_iota(jnp.int32, (ENS, LANES), 1)
    repeated = exact_dot(mix, jnp.where(lax.rem(ec, ENS) == er, 1.0, 0.0))
    full = jnp.concatenate([repeated] * 4, axis=0)
    br = lax.broadcasted_iota(jnp.int32, (LANES, LANES), 0) // ENS
    bc = lax.broadcasted_iota(jnp.int32, (LANES, LANES), 1) // ENS
    out_ref[...] = jnp.where(br == bc, full, 0.0)


def tile_mix(tiles_east, tiles_north, sums):
    tiles = tiles_east * tiles_north
    return pl.pallas_call(
        functools.partial(mix_kernel, tiles_east, tiles_north),
        out_shape=jax.ShapeDtypeStruct((LANES, LANES), F32),
        in_specs=[vmem],
        out_specs=vmem,
        scratch_shapes=[
            pltpu.VMEM((tiles - 1, 9, LANES), F32),
            pltpu.SemaphoreType.DMA,
            pltpu.SemaphoreType.DMA,
        ],
        compiler_params=pltpu.CompilerParams(
            collective_id=0, has_side_effects=True, vmem_limit_bytes=VMEM_LIMIT
        ),
    )(sums)


def apply_kernel(field_ref, one_ref, two_ref, out_ref):
    high, low = split(exact_dot(one_ref[...], two_ref[...]))
    both = jnp.concatenate(
        [jnp.concatenate([high, low], axis=1), jnp.concatenate([high, jnp.zeros_like(low)], axis=1)], axis=0
    )
    for comp in range(COMP):
        lanes = slice(comp * LANES, (comp + 1) * LANES)
        result = half_dot(jnp.concatenate(split(field_ref[:, lanes]), axis=1), both)
        out_ref[:, lanes] = result[:, 0:LANES] + result[:, LANES:]


def apply_mix(field, one, two):
    rows, feat = field.shape
    block = 512
    return pl.pallas_call(
        apply_kernel,
        out_shape=jax.ShapeDtypeStruct((rows, feat), F32),
        grid=(rows // block,),
        in_specs=[
            pl.BlockSpec((block, feat), lambda i: (i, 0)),
            pl.BlockSpec((LANES, LANES), lambda i: (0, 0)),
            pl.BlockSpec((LANES, LANES), lambda i: (0, 0)),
        ],
        out_specs=pl.BlockSpec((block, feat), lambda i: (i, 0)),
        compiler_params=pltpu.CompilerParams(vmem_limit_bytes=VMEM_LIMIT),
    )(field, one, two)


def neighbours(axis, last, initial):
    size = lax.axis_size(axis)
    up = [(i, (i + 1) % size) for i in range(size)]
    down = [(j, i) for i, j in up]
    return lax.ppermute(last, axis, up), lax.ppermute(initial, axis, down)


def table_kernel(
    nx, ny, tiles_east, tiles_north, blocks,
    owner_in, cell_in, level_in, coef_in, value_in, error_in, pattern_ref, out_ref,
    owner_ref, cell_ref, level_ref, coef_ref, value_ref, error_ref, copied,
):
    far = (owner_in, cell_in, level_in, coef_in, value_in, error_in)
    near = (owner_ref, cell_ref, level_ref, coef_ref, value_ref, error_ref)
    copies = [pltpu.make_async_copy(a, b, copied.at[i]) for i, (a, b) in enumerate(zip(far, near))]
    for copy in copies:
        copy.start()
    for copy in copies:
        copy.wait()
    tiles = tiles_east * tiles_north
    nobs = owner_ref.shape[1]
    width = out_ref.shape[1]
    grid_east, grid_north = float(nx * tiles_east), float(ny * tiles_north)

    def parts(value, size):
        whole = jnp.floor((value + 0.5) * (1.0 / size))
        return whole, value - whole * size

    tile = lax.broadcasted_iota(jnp.int32, (tiles, LANES), 0).astype(F32)
    tile_east, tile_north = parts(tile, tiles_north)
    centre_east = tile_east * nx + (nx - 1) / 2.0
    centre_north = tile_north * ny + (ny - 1) / 2.0
    lane = lax.broadcasted_iota(jnp.int32, (tiles, LANES), 1)

    def scaled(place, centre, grid):
        gap = place - centre
        gap = jnp.where(gap >= grid / 2.0, gap - grid, gap)
        gap = jnp.where(gap < -grid / 2.0, gap + grid, gap)
        return gap * (1.0 / (radius_share * grid))

    def one(c, carry):
        at = pl.ds(pl.multiple_of(c * LANES, LANES), LANES)
        columns, rhos = [], []
        for batch in range(2):
            row = slice(batch, batch + 1)
            owner_east, owner_north = parts(owner_ref[row, at].astype(F32), tiles_north)
            cell_east, cell_north = parts(cell_ref[row, at].astype(F32), ny)
            far_east = scaled(owner_east * nx + cell_east, centre_east, grid_east)
            far_north = scaled(owner_north * ny + cell_north, centre_north, grid_north)
            used = batch * blocks + (c * LANES) // (nobs // blocks)
            mask = jnp.sum(jnp.where(lane == used, pattern_ref[...], 0.0), axis=1, keepdims=True)
            rhos.append(mask * jnp.exp(-0.5 * (far_east * far_east + far_north * far_north)))
            columns += [
                coef_ref[batch, :, at],
                level_ref[row, at].astype(F32),
                value_ref[row, at],
                1.0 / error_ref[row, at],
                jnp.zeros((2, LANES), F32),
            ]
        spare = jnp.zeros((width - 16 - 2 * tiles, LANES), F32)
        out_ref[at, :] = jnp.concatenate([*columns, *rhos, spare], axis=0).T
        return carry

    lax.fori_loop(0, nobs // LANES, one, 0)


def make_table(nx, ny, tiles_east, tiles_north, blocks, patterns, owner, cell, level, coef, value, error):
    tiles = tiles_east * tiles_north
    nobs = owner.shape[1]
    width = -(-(16 + 2 * tiles) // LANES) * LANES
    return pl.pallas_call(
        functools.partial(table_kernel, nx, ny, tiles_east, tiles_north, blocks),
        out_shape=jax.ShapeDtypeStruct((nobs, width), F32),
        in_specs=[pl.BlockSpec(memory_space=pltpu.HBM)] * 6 + [vmem],
        out_specs=vmem,
        scratch_shapes=[
            pltpu.VMEM(owner.shape, jnp.int32),
            pltpu.VMEM(cell.shape, jnp.int32),
            pltpu.VMEM(level.shape, jnp.int32),
            pltpu.VMEM(coef.shape, F32),
            pltpu.VMEM(value.shape, F32),
            pltpu.VMEM(error.shape, F32),
            pltpu.SemaphoreType.DMA((6,)),
        ],
        compiler_params=pltpu.CompilerParams(vmem_limit_bytes=62 * 1024 * 1024),
        cost_estimate=pl.CostEstimate(flops=50_000_000, bytes_accessed=12_000_000, transcendentals=0),
    )(owner, cell, level, coef, value, error, patterns.reshape(tiles, LANES))


def local(state, obs_owner, obs_cell, obs_level, obs_coef, obs_value, obs_error, pattern):
    span_east, span_north, features = state.shape
    tiles_east = lax.axis_size("gx")
    tiles_north = lax.axis_size("gy")
    tiles = tiles_east * tiles_north
    nobs = obs_owner.shape[1]

    west, east = neighbours("gx", state[-2:], state[:2])
    patterns, lists = prepare(tiles_east, tiles_north, pattern[0, 0], obs_owner)
    last = jnp.concatenate([west[:, -2:], state[:, -2:], east[:, -2:]], axis=0)
    initial = jnp.concatenate([west[:, :2], state[:, :2], east[:, :2]], axis=0)
    last, initial, patterns = lax.optimization_barrier((last, initial, patterns))
    south, north = neighbours("gy", last, initial)
    cells = obs_cell
    table = make_table(
        span_east, span_north, tiles_east, tiles_north, pattern.shape[3], patterns,
        obs_owner, obs_cell, obs_level, obs_coef, obs_value, obs_error,
    )

    field = forecast(state, west, east, south, north)
    sums = own_sums(0, nobs, tiles, lists, cells, field, table)
    first_mix = tile_mix(tiles_east, tiles_north, sums)
    sums = own_sums(1, nobs, tiles, lists, cells, field, table, first_mix)
    second_mix = tile_mix(tiles_east, tiles_north, sums)
    return apply_mix(field, first_mix, second_mix).reshape(span_east, span_north, features)


def solution(mesh):
    placed = (P("gx", "gy", None), P(), P(), P(), P(), P(), P(), P("gx", "gy", None, None))
    return jax.shard_map(
        local, mesh=mesh, in_specs=placed, out_specs=P("gx", "gy", None), check_vma=False
    )
```

```python
import functools
import math

import jax
import jax.numpy as jnp
from jax import lax
from jax.experimental import pallas as pl
from jax.experimental.pallas import tpu as pltpu
from jax.sharding import PartitionSpec as P

ENS = 32
LEV = 4
COMP = 3
NSIT = 4
CHUNK = 256
LANES = 128

courant = 0.1
diffusion = 0.08
radius_share = 0.25

VMEM_LIMIT = 48 * 1024 * 1024
HIGHEST = lax.Precision.HIGHEST
F32 = jnp.float32
BF16 = jnp.bfloat16

smem = pl.BlockSpec(memory_space=pltpu.SMEM)
vmem = pl.BlockSpec(memory_space=pltpu.VMEM)


def exact_dot(left, right):
    return jnp.dot(left, right, precision=HIGHEST, preferred_element_type=F32)


def half_dot(left, right):
    return jnp.dot(left, right, preferred_element_type=F32)


def split(values):
    high = values.astype(BF16)
    low = (values - high.astype(F32)).astype(BF16)
    return high, low


def prepare_kernel(tiles_east, tiles_north, pattern_ref, owner_ref, all_ref, list_ref, raw, ranks, held, send_sem, recv_sem):
    tiles = tiles_east * tiles_north
    me = lax.axis_index("gx") * tiles_north + lax.axis_index("gy")

    def device(t):
        return (t // tiles_north, lax.rem(t, tiles_north))

    barrier = pltpu.get_barrier_semaphore()

    def greet(d, carry):
        pl.semaphore_signal(
            barrier, inc=1, device_id=device(lax.rem(me + d, tiles)), device_id_type=pl.DeviceIdType.MESH
        )
        return carry

    lax.fori_loop(1, tiles, greet, 0)
    groups = owner_ref.shape[1] // LANES
    for c in range(groups):
        for batch in range(2):
            raw[batch * groups + c : batch * groups + c + 1, :] = owner_ref[
                batch : batch + 1, c * LANES : (c + 1) * LANES
            ]
    pl.semaphore_wait(barrier, tiles - 1)

    def send(d, carry):
        pltpu.make_async_remote_copy(
            src_ref=pattern_ref,
            dst_ref=held.at[d - 1],
            send_sem=send_sem,
            recv_sem=recv_sem,
            device_id=device(lax.rem(me + d, tiles)),
            device_id_type=pl.DeviceIdType.MESH,
        ).start()
        return carry

    lax.fori_loop(1, tiles, send, 0)

    rows = list_ref.shape[0]
    sub = lax.broadcasted_iota(jnp.int32, (LANES, LANES), 0)
    lane = lax.broadcasted_iota(jnp.int32, (LANES, LANES), 1)
    mine = jnp.where(raw[...] == me, 1.0, 0.0)
    before = jnp.where(sub < lane, 1.0, 0.0).astype(BF16)
    ranks[...] = jnp.where(mine > 0.5, half_dot(mine.astype(BF16), before), -1.0)
    place = lax.broadcasted_iota(jnp.int32, (16, LANES), 1).astype(F32).astype(BF16)
    slot = sub.astype(F32)

    def listed(i, carry):
        block = ranks[pl.ds(pl.multiple_of(i * 8, 8), 8), :]
        found = []
        for k in range(8):
            hot = jnp.where(block[k : k + 1] == slot, 1.0, 0.0).astype(BF16)
            found.append(
                lax.dot_general(place, hot, (((1,), (1,)), ((), ())), preferred_element_type=F32)[0:1]
            )
        rows8 = jnp.concatenate(found, axis=0)
        number = jnp.sum(jnp.where(block >= 0.0, 1.0, 0.0), axis=1, keepdims=True)
        list_ref[pl.ds(pl.multiple_of(i * 8, 8), 8), :] = (rows8 + 256.0 * number).astype(jnp.int32)
        return carry

    lax.fori_loop(0, rows // 8, listed, 0)
    all_ref[me] = pattern_ref[...]
    pltpu.make_async_copy(held, held, recv_sem).wait()
    pltpu.make_async_copy(held, held, send_sem).wait()

    def place_one(d, carry):
        all_ref[lax.rem(me - d + tiles, tiles)] = held[d - 1]
        return carry

    lax.fori_loop(1, tiles, place_one, 0)


def prepare(tiles_east, tiles_north, pattern, owners):
    tiles = tiles_east * tiles_north
    flat = pattern.reshape(1, -1).astype(F32)
    flat = jnp.pad(flat, ((0, 0), (0, LANES - flat.shape[1])))
    rows = (owners.size // LANES, LANES)
    return pl.pallas_call(
        functools.partial(prepare_kernel, tiles_east, tiles_north),
        out_shape=(
            jax.ShapeDtypeStruct((tiles, 1, LANES), F32),
            jax.ShapeDtypeStruct(rows, jnp.int32),
        ),
        in_specs=[vmem, vmem],
        out_specs=(vmem, vmem),
        scratch_shapes=[
            pltpu.VMEM(rows, jnp.int32),
            pltpu.VMEM(rows, F32),
            pltpu.VMEM((tiles - 1, 1, LANES), F32),
            pltpu.SemaphoreType.DMA,
            pltpu.SemaphoreType.DMA,
        ],
        compiler_params=pltpu.CompilerParams(collective_id=1, has_side_effects=True),
    )(flat, owners)


def forecast_kernel(state_ref, west_ref, east_ref, south_ref, north_ref, out_ref, wide, middle):
    nx, ny, _ = state_ref.shape
    wide[2 : nx + 2, 8 : ny + 8, :] = state_ref[...]
    wide[0:2, 8 : ny + 8, :] = west_ref[...]
    wide[nx + 2 : nx + 4, 8 : ny + 8, :] = east_ref[...]
    wide[:, 6:8, :] = south_ref[...]
    wide[:, ny + 8 : ny + 10, :] = north_ref[...]
    rows = ny + 16

    def updated(src, x, comp, up, um, vp, vm):
        lanes = slice(comp * LANES, (comp + 1) * LANES)
        centre = src[x, :, lanes]
        west = src[x - 1, :, lanes]
        east = src[x + 1, :, lanes]
        south = pltpu.roll(centre, 1, 0)
        north = pltpu.roll(centre, rows - 1, 0)
        along = um * (east - centre) - up * (centre - west)
        across = vm * (north - centre) - vp * (centre - south)
        return centre + (along + across)

    def speeds(src, x):
        u = src[x, :, 0:LANES]
        v = src[x, :, LANES : 2 * LANES]
        return (
            diffusion + courant * jnp.maximum(u, 0.0),
            diffusion - courant * jnp.minimum(u, 0.0),
            diffusion + courant * jnp.maximum(v, 0.0),
            diffusion - courant * jnp.minimum(v, 0.0),
        )

    def first(i, carry):
        parts = speeds(wide, i + 1)
        for comp in range(COMP):
            middle[i, :, comp * LANES : (comp + 1) * LANES] = updated(wide, i + 1, comp, *parts)
        return carry

    lax.fori_loop(0, nx + 2, first, 0)

    def second(i, carry):
        parts = speeds(middle, i + 1)
        for comp in range(COMP):
            new = updated(middle, i + 1, comp, *parts)
            out_ref[pl.ds(pl.multiple_of(i * ny, ny), ny), comp * LANES : (comp + 1) * LANES] = new[8 : ny + 8]
        return carry

    lax.fori_loop(0, nx, second, 0)


def forecast(state, west, east, south, north):
    nx, ny, feat = state.shape
    return pl.pallas_call(
        forecast_kernel,
        out_shape=jax.ShapeDtypeStruct((nx * ny, feat), F32),
        in_specs=[vmem] * 5,
        out_specs=vmem,
        scratch_shapes=[
            pltpu.VMEM((nx + 4, ny + 16, feat), F32),
            pltpu.VMEM((nx + 2, ny + 16, feat), F32),
        ],
        compiler_params=pltpu.CompilerParams(vmem_limit_bytes=VMEM_LIMIT),
    )(state, west, east, south, north)


def sums_kernel(batch, nobs, tiles, mixed, list_ref, cell_ref, field_ref, table_ref, *rest):
    if mixed:
        mix_ref, out_ref, picked, params, total = rest
    else:
        out_ref, picked, params, total = rest
    blocks = nobs // LANES
    total[...] = jnp.zeros_like(total)
    lane = lax.broadcasted_iota(jnp.int32, (CHUNK, LANES), 1)
    group = lane // ENS
    row = lax.broadcasted_iota(jnp.int32, (CHUNK, 1), 0)
    first_lane = 16 + batch * tiles

    def block_of(c, start):
        number = lax.shift_right_logical(list_ref[batch * blocks + c, 0], 8)

        def pick(i, carry):
            js = [c * LANES + (list_ref[batch * blocks + c, i * 8 + k] & 255) for k in range(8)]
            values = [field_ref[pl.ds(cell_ref[batch * nobs + j], 1), :] for j in js]
            entries = [table_ref[pl.ds(j, 1), :] for j in js]
            for k in range(8):
                picked[pl.ds(start + i * 8 + k, 1), :] = values[k]
                params[pl.ds(start + i * 8 + k, 1), :] = entries[k]
            return carry

        lax.fori_loop(0, lax.shift_right_logical(number + 7, 3), pick, 0)
        return start + number

    count = lax.fori_loop(0, blocks, block_of, 0)

    def chunk(ci, carry):
        rows = pl.ds(pl.multiple_of(ci * CHUNK, CHUNK), CHUNK)
        valid = ci * CHUNK + row < count
        param = jnp.where(valid, params[rows, 0:LANES], 0.0)
        column = batch * 8
        values = (
            param[:, column : column + 1] * picked[rows, 0:LANES]
            + param[:, column + 1 : column + 2] * picked[rows, LANES : 2 * LANES]
            + param[:, column + 2 : column + 3] * picked[rows, 2 * LANES : 3 * LANES]
        )
        values = jnp.where(valid & (group.astype(F32) == param[:, column + 3 : column + 4]), values, 0.0)
        values = values + pltpu.roll(values, 64, 1)
        values = values + pltpu.roll(values, 32, 1)
        if mixed:
            values = exact_dot(values, mix_ref[...])
        centre = jnp.sum(values, axis=1, keepdims=True) / float(LANES)
        inverse_error = param[:, column + 5 : column + 6]
        deviation = (values - centre) * inverse_error
        innovation = (param[:, column + 4 : column + 5] - centre) * inverse_error
        left = jnp.where(group == 0, deviation, jnp.where(lane == ENS, innovation, 0.0))
        high, low = split(left.T[0:48])
        both = jnp.concatenate([high, low], axis=0)
        pair = jnp.concatenate([deviation, deviation], axis=1)
        for g in range(tiles // 8):
            spread = []
            for h in range(2):
                column = first_lane + g * 8 + h * 4
                whole, inside = column // LANES, column % LANES
                source = param if whole == 0 else jnp.where(
                    valid, params[rows, whole * LANES : (whole + 1) * LANES], 0.0
                )
                spread.append(jnp.take_along_axis(source, group + inside, axis=1, mode="promise_in_bounds"))
            weight = jnp.concatenate(spread, axis=1)
            right_high, right_low = split(weight * pair)
            first = half_dot(both, right_high)
            second = half_dot(high, right_low)
            total[:, g * 256 : (g + 1) * 256] += first[0:48] + first[48:96] + second
        return carry

    lax.fori_loop(0, (count + CHUNK - 1) // CHUNK, chunk, 0)
    small = lax.broadcasted_iota(jnp.int32, (8, LANES), 1) // ENS

    def pack(q, carry):
        lanes = pl.ds(pl.multiple_of(q * LANES, LANES), LANES)
        blocks = [total[8 * r : 8 * r + 8, lanes] for r in range(5)]
        for t in range(4):
            packed = jnp.zeros((8, LANES), F32)
            for r in range(4):
                moved = pltpu.roll(blocks[r], (32 * (r - t)) % LANES, 1) if r != t else blocks[r]
                packed = jnp.where(small == r, moved, packed)
            proj = pltpu.roll(blocks[4], (-32 * t) % LANES, 1) if t else blocks[4]
            out_ref[q * 4 + t, 0:8, :] = packed
            out_ref[q * 4 + t, 8:9, :] = jnp.where(small == 0, proj, 0.0)[0:1]
        return carry

    lax.fori_loop(0, tiles // 4, pack, 0)


def own_sums(batch, nobs, tiles, lists, cells, field, table, mix=None):
    extra = [] if mix is None else [mix]
    return pl.pallas_call(
        functools.partial(sums_kernel, batch, nobs, tiles, mix is not None),
        out_shape=jax.ShapeDtypeStruct((tiles, 9, LANES), F32),
        in_specs=[smem] * 2 + [vmem] * (2 + len(extra)),
        out_specs=vmem,
        scratch_shapes=[
            pltpu.VMEM((nobs + 8, COMP * LANES), F32),
            pltpu.VMEM((nobs + 8, table.shape[1]), F32),
            pltpu.VMEM((48, tiles * ENS), F32),
        ],
        compiler_params=pltpu.CompilerParams(vmem_limit_bytes=VMEM_LIMIT),
    )(lists, cells, field, table, *extra)


def mix_kernel(tiles_east, tiles_north, x_ref, out_ref, held, send_sem, recv_sem):
    tiles = tiles_east * tiles_north
    me = lax.axis_index("gx") * tiles_north + lax.axis_index("gy")

    def device(t):
        return (t // tiles_north, lax.rem(t, tiles_north))

    barrier = pltpu.get_barrier_semaphore()

    def greet(d, carry):
        pl.semaphore_signal(
            barrier, inc=1, device_id=device(lax.rem(me + d, tiles)), device_id_type=pl.DeviceIdType.MESH
        )
        return carry

    lax.fori_loop(1, tiles, greet, 0)
    pl.semaphore_wait(barrier, tiles - 1)

    def send(d, carry):
        target = lax.rem(me + d, tiles)
        pltpu.make_async_remote_copy(
            src_ref=x_ref.at[target],
            dst_ref=held.at[d - 1],
            send_sem=send_sem,
            recv_sem=recv_sem,
            device_id=device(target),
            device_id_type=pl.DeviceIdType.MESH,
        ).start()
        return carry

    lax.fori_loop(1, tiles, send, 0)
    pltpu.make_async_copy(held, held, recv_sem).wait()
    pltpu.make_async_copy(held, held, send_sem).wait()

    total = x_ref[me] + jnp.sum(held[...], axis=0)
    top = total[0:8]
    cov = jnp.concatenate([top] + [pltpu.roll(top, LANES - 32 * r, 1) for r in range(1, 4)], axis=0)[:, 0:ENS]
    proj = total[8:9, 0:ENS]
    ri = lax.broadcasted_iota(jnp.int32, (ENS, ENS), 0)
    ci = lax.broadcasted_iota(jnp.int32, (ENS, ENS), 1)
    unit = jnp.where(ri == ci, 1.0, 0.0)
    system = (ENS - 1.0) * unit + cov
    bound = jnp.max(jnp.sum(jnp.abs(system), axis=1, keepdims=True), axis=0, keepdims=True)
    approach, root = system / bound, unit
    middle = 1.5 * unit - 0.5 * approach
    approach, root = exact_dot(approach, middle), middle
    for sweep in range(1, NSIT):
        middle = 1.5 * unit - 0.5 * exact_dot(root, approach)
        if sweep < NSIT - 1:
            approach = exact_dot(approach, middle)
        root = exact_dot(middle, root)
    inverse = exact_dot(root, root) / bound
    weights = jnp.sum(inverse * proj, axis=1, keepdims=True)
    shifts = weights + math.sqrt(ENS - 1.0) * root / jnp.sqrt(bound)
    mix = 1.0 / ENS + (shifts - jnp.mean(shifts, axis=0, keepdims=True))
    er = lax.broadcasted_iota(jnp.int32, (ENS, LANES), 0)
    ec = lax.broadcasted_iota(jnp.int32, (ENS, LANES), 1)
    repeated = exact_dot(mix, jnp.where(lax.rem(ec, ENS) == er, 1.0, 0.0))
    full = jnp.concatenate([repeated] * 4, axis=0)
    br = lax.broadcasted_iota(jnp.int32, (LANES, LANES), 0) // ENS
    bc = lax.broadcasted_iota(jnp.int32, (LANES, LANES), 1) // ENS
    out_ref[...] = jnp.where(br == bc, full, 0.0)


def tile_mix(tiles_east, tiles_north, sums):
    tiles = tiles_east * tiles_north
    return pl.pallas_call(
        functools.partial(mix_kernel, tiles_east, tiles_north),
        out_shape=jax.ShapeDtypeStruct((LANES, LANES), F32),
        in_specs=[vmem],
        out_specs=vmem,
        scratch_shapes=[
            pltpu.VMEM((tiles - 1, 9, LANES), F32),
            pltpu.SemaphoreType.DMA,
            pltpu.SemaphoreType.DMA,
        ],
        compiler_params=pltpu.CompilerParams(
            collective_id=0, has_side_effects=True, vmem_limit_bytes=VMEM_LIMIT
        ),
    )(sums)


def apply_kernel(field_ref, one_ref, two_ref, out_ref):
    high, low = split(exact_dot(one_ref[...], two_ref[...]))
    both = jnp.concatenate(
        [jnp.concatenate([high, low], axis=1), jnp.concatenate([high, jnp.zeros_like(low)], axis=1)], axis=0
    )
    for comp in range(COMP):
        lanes = slice(comp * LANES, (comp + 1) * LANES)
        result = half_dot(jnp.concatenate(split(field_ref[:, lanes]), axis=1), both)
        out_ref[:, lanes] = result[:, 0:LANES] + result[:, LANES:]


def apply_mix(field, one, two):
    rows, feat = field.shape
    block = 512
    return pl.pallas_call(
        apply_kernel,
        out_shape=jax.ShapeDtypeStruct((rows, feat), F32),
        grid=(rows // block,),
        in_specs=[
            pl.BlockSpec((block, feat), lambda i: (i, 0)),
            pl.BlockSpec((LANES, LANES), lambda i: (0, 0)),
            pl.BlockSpec((LANES, LANES), lambda i: (0, 0)),
        ],
        out_specs=pl.BlockSpec((block, feat), lambda i: (i, 0)),
        compiler_params=pltpu.CompilerParams(vmem_limit_bytes=VMEM_LIMIT),
    )(field, one, two)


def neighbours(axis, last, initial):
    size = lax.axis_size(axis)
    up = [(i, (i + 1) % size) for i in range(size)]
    down = [(j, i) for i, j in up]
    return lax.ppermute(last, axis, up), lax.ppermute(initial, axis, down)


def table_kernel(
    nx, ny, tiles_east, tiles_north, blocks,
    owner_in, cell_in, level_in, coef_in, value_in, error_in, pattern_ref, out_ref,
    owner_ref, cell_ref, level_ref, coef_ref, value_ref, error_ref, copied,
):
    far = (owner_in, cell_in, level_in, coef_in, value_in, error_in)
    near = (owner_ref, cell_ref, level_ref, coef_ref, value_ref, error_ref)
    copies = [pltpu.make_async_copy(a, b, copied.at[i]) for i, (a, b) in enumerate(zip(far, near))]
    for copy in copies:
        copy.start()
    for copy in copies:
        copy.wait()
    tiles = tiles_east * tiles_north
    nobs = owner_ref.shape[1]
    width = out_ref.shape[1]
    grid_east, grid_north = float(nx * tiles_east), float(ny * tiles_north)

    def parts(value, size):
        whole = jnp.floor((value + 0.5) * (1.0 / size))
        return whole, value - whole * size

    tile = lax.broadcasted_iota(jnp.int32, (tiles, LANES), 0).astype(F32)
    tile_east, tile_north = parts(tile, tiles_north)
    centre_east = tile_east * nx + (nx - 1) / 2.0
    centre_north = tile_north * ny + (ny - 1) / 2.0
    lane = lax.broadcasted_iota(jnp.int32, (tiles, LANES), 1)

    def scaled(place, centre, grid):
        gap = place - centre
        gap = jnp.where(gap >= grid / 2.0, gap - grid, gap)
        gap = jnp.where(gap < -grid / 2.0, gap + grid, gap)
        return gap * (1.0 / (radius_share * grid))

    def one(c, carry):
        at = pl.ds(pl.multiple_of(c * LANES, LANES), LANES)
        columns, rhos = [], []
        for batch in range(2):
            row = slice(batch, batch + 1)
            owner_east, owner_north = parts(owner_ref[row, at].astype(F32), tiles_north)
            cell_east, cell_north = parts(cell_ref[row, at].astype(F32), ny)
            far_east = scaled(owner_east * nx + cell_east, centre_east, grid_east)
            far_north = scaled(owner_north * ny + cell_north, centre_north, grid_north)
            used = batch * blocks + (c * LANES) // (nobs // blocks)
            mask = jnp.sum(jnp.where(lane == used, pattern_ref[...], 0.0), axis=1, keepdims=True)
            rhos.append(mask * jnp.exp(-0.5 * (far_east * far_east + far_north * far_north)))
            columns += [
                coef_ref[batch, :, at],
                level_ref[row, at].astype(F32),
                value_ref[row, at],
                1.0 / error_ref[row, at],
                jnp.zeros((2, LANES), F32),
            ]
        spare = jnp.zeros((width - 16 - 2 * tiles, LANES), F32)
        out_ref[at, :] = jnp.concatenate([*columns, *rhos, spare], axis=0).T
        return carry

    lax.fori_loop(0, nobs // LANES, one, 0, unroll=4)


def make_table(nx, ny, tiles_east, tiles_north, blocks, patterns, owner, cell, level, coef, value, error):
    tiles = tiles_east * tiles_north
    nobs = owner.shape[1]
    width = -(-(16 + 2 * tiles) // LANES) * LANES
    return pl.pallas_call(
        functools.partial(table_kernel, nx, ny, tiles_east, tiles_north, blocks),
        out_shape=jax.ShapeDtypeStruct((nobs, width), F32),
        in_specs=[pl.BlockSpec(memory_space=pltpu.HBM)] * 6 + [vmem],
        out_specs=vmem,
        scratch_shapes=[
            pltpu.VMEM(owner.shape, jnp.int32),
            pltpu.VMEM(cell.shape, jnp.int32),
            pltpu.VMEM(level.shape, jnp.int32),
            pltpu.VMEM(coef.shape, F32),
            pltpu.VMEM(value.shape, F32),
            pltpu.VMEM(error.shape, F32),
            pltpu.SemaphoreType.DMA((6,)),
        ],
        compiler_params=pltpu.CompilerParams(vmem_limit_bytes=62 * 1024 * 1024),
        cost_estimate=pl.CostEstimate(flops=50_000_000, bytes_accessed=12_000_000, transcendentals=0),
    )(owner, cell, level, coef, value, error, patterns.reshape(tiles, LANES))


def local(state, obs_owner, obs_cell, obs_level, obs_coef, obs_value, obs_error, pattern):
    span_east, span_north, features = state.shape
    tiles_east = lax.axis_size("gx")
    tiles_north = lax.axis_size("gy")
    tiles = tiles_east * tiles_north
    nobs = obs_owner.shape[1]

    west, east = neighbours("gx", state[-2:], state[:2])
    patterns, lists = prepare(tiles_east, tiles_north, pattern[0, 0], obs_owner)
    last = jnp.concatenate([west[:, -2:], state[:, -2:], east[:, -2:]], axis=0)
    initial = jnp.concatenate([west[:, :2], state[:, :2], east[:, :2]], axis=0)
    last, initial, patterns = lax.optimization_barrier((last, initial, patterns))
    south, north = neighbours("gy", last, initial)
    cells = obs_cell.reshape(-1)
    table = make_table(
        span_east, span_north, tiles_east, tiles_north, pattern.shape[3], patterns,
        obs_owner, obs_cell, obs_level, obs_coef, obs_value, obs_error,
    )

    field = forecast(state, west, east, south, north)
    sums = own_sums(0, nobs, tiles, lists, cells, field, table)
    first_mix = tile_mix(tiles_east, tiles_north, sums)
    sums = own_sums(1, nobs, tiles, lists, cells, field, table, first_mix)
    second_mix = tile_mix(tiles_east, tiles_north, sums)
    return apply_mix(field, first_mix, second_mix).reshape(span_east, span_north, features)


def solution(mesh):
    placed = (P("gx", "gy", None), P(), P(), P(), P(), P(), P(), P("gx", "gy", None, None))
    return jax.shard_map(
        local, mesh=mesh, in_specs=placed, out_specs=P("gx", "gy", None), check_vma=False
    )
```
